512 devices in a mesh: blk: 8 (over z_lo, core), grp: 64 (over y, z_hi, x).
Axes of the slice: x: 4, y: 8, z: 8 (z_hi: 2, z_lo: 4; z = z_hi * 4 + z_lo), core: 2. Of those that a mesh axis runs over, the one named last changes fastest.
Arguments:
- picture_inputs: bfloat16 [65536, 768], P(('blk', 'grp')), may hold values from -6 to 6
- caption_inputs: bfloat16 [65536, 768], P(('blk', 'grp')), may hold values from -6 to 6
- picture_mapping: bfloat16 [768, 768], P('grp'), may hold values from -0.21875 to 0.21875
- caption_mapping: bfloat16 [768, 768], P('grp'), may hold values from -0.21875 to 0.21875
- similarity_multiplier: float32 [1], replicated, may hold values from 2 to 8
- score_constant: float32 [1], replicated, may hold values from -6 to -3
Outputs:
- img_proj_grad: float32 [768, 768], P('grp')
- txt_proj_grad: float32 [768, 768], P('grp')
- img_norms: float32 [65536], P(('blk', 'grp'))
- txt_norms: float32 [65536], P(('blk', 'grp'))
The draws below stay inside these ranges and needn't reach their ends.
All inputs are finite; a program needn't handle non-finite values.
Results may differ from the reference program's by a relative error of at most 0.0036.
Values may be sent and summed in bfloat16 or wider, within the bound.
No kernel may reach another device: no remote copies, remote signals or barrier semaphores. Data moves between devices by JAX's collectives and lax.ppermute only.
A program may use at most 64 MiB of HBM per device.

```python
import math
import jax
import jax.numpy as jnp
from jax import lax

WIDTH = 768
EMBED = 768
ROWS_DEV = 128
SET = 1024
BATCH = 65536
N_BLK = 8
N_GRP = 64


def block_scale(key, shape, cuts, least, high):
    loudness = 1.0
    for position, parts in cuts:
        draws = jax.random.uniform(jax.random.fold_in(jax.random.fold_in(key, 6), position), (parts,), jnp.float32, least / len(cuts), high / len(cuts))
        loudness = loudness * jnp.repeat(jnp.exp(draws), shape[position] // parts).reshape((-1,) + (1,) * (len(shape) - 1 - position))
    return loudness


def bell_draw(stream_key, shape, spread, bound, shards=(), held_as=jnp.bfloat16):
    result = jax.random.normal(stream_key, shape, jnp.float32) * spread
    if len(shards) > 0:
        result = block_scale(stream_key, shape, shards, -0.22, 0.18) * result
    return jnp.clip(result, min=-bound, max=bound).astype(held_as)


def setup_inputs(seed: int = 0) -> dict:
    seeds = jax.random.split(jax.random.key(seed), 7)
    return {
        "picture_inputs": bell_draw(seeds[0], (BATCH, WIDTH), 1.0, 6.0, ((0, 512),)),
        "caption_inputs": bell_draw(seeds[1], (BATCH, WIDTH), 1.0, 6.0, ((0, 512),)),
        "picture_mapping": bell_draw(seeds[2], (WIDTH, EMBED), WIDTH ** -0.5, 0.21875, ((0, 64),)),
        "caption_mapping": bell_draw(seeds[3], (WIDTH, EMBED), WIDTH ** -0.5, 0.21875, ((0, 64),)),
        "similarity_multiplier": jnp.clip(jnp.exp(jax.random.uniform(seeds[4], (1,), jnp.float32, math.log(2.0), math.log(8.0))), 2.0, 8.0),
        "score_constant": jnp.clip(jax.random.uniform(seeds[5], (1,), jnp.float32, -6.0, -3.0), -6.0, -3.0),
    }


def unit_rows(projected):
    radius = jnp.sqrt(lax.optimization_barrier(jnp.sum(projected * projected, axis=-1, keepdims=True)) + 1e-06)
    return (projected / radius, radius)

def through_norm(unit, radius, upstream):
    return (upstream - unit * lax.optimization_barrier(jnp.sum(unit * upstream, axis=-1, keepdims=True))) / radius

def to_sets(values):
    return values.reshape(N_BLK, N_GRP, ROWS_DEV, EMBED).transpose(1, 0, 2, 3).reshape(N_GRP, SET, EMBED)

def from_sets(values):
    return values.reshape(N_GRP, N_BLK, ROWS_DEV, EMBED).transpose(1, 0, 2, 3).reshape(BATCH, EMBED)

def reference(picture_inputs, caption_inputs, picture_mapping, caption_mapping, similarity_multiplier, score_constant):
    img_out = jnp.dot(picture_inputs, picture_mapping, preferred_element_type=jnp.float32)
    txt_out = jnp.dot(caption_inputs, caption_mapping, preferred_element_type=jnp.float32)
    img_unit, img_radius = unit_rows(img_out)
    txt_unit, txt_radius = unit_rows(txt_out)
    img_half = img_unit.astype(jnp.bfloat16)
    text_half = txt_unit.astype(jnp.bfloat16)
    multiplier_amount = similarity_multiplier[0]
    set_offset = score_constant[0]
    set_ids = jnp.arange(SET, dtype=jnp.int32)
    pair_label_sign = jnp.where(set_ids[:, None] == set_ids[None, :], 1.0, -1.0).astype(jnp.float32)

    def one_set(pair):
        image_set_rows, text_set_rows = pair
        pair_logits = multiplier_amount * jnp.dot(image_set_rows, text_set_rows.T, preferred_element_type=jnp.float32) + set_offset
        weight_matrices = (-multiplier_amount * pair_label_sign * jax.nn.sigmoid(-pair_label_sign * pair_logits)).astype(jnp.bfloat16)
        img_part = jnp.dot(weight_matrices, text_set_rows, preferred_element_type=jnp.float32)
        txt_part = lax.dot_general(weight_matrices, image_set_rows, (((0,), (0,)), ((), ())), preferred_element_type=jnp.float32)
        return (img_part, txt_part)
    img_grad, txt_grad = lax.map(one_set, (to_sets(img_half), to_sets(text_half)))
    img_grad = from_sets(img_grad)
    txt_grad = from_sets(txt_grad)
    img_pre = through_norm(img_unit, img_radius, img_grad)
    txt_pre = through_norm(txt_unit, txt_radius, txt_grad)
    img_proj_grad = jnp.dot(picture_inputs.T, img_pre.astype(jnp.bfloat16), preferred_element_type=jnp.float32)
    txt_proj_grad = jnp.dot(caption_inputs.T, txt_pre.astype(jnp.bfloat16), preferred_element_type=jnp.float32)
    img_wide = picture_inputs.astype(jnp.float32)
    txt_wide = caption_inputs.astype(jnp.float32)
    img_norms = jnp.sqrt(lax.optimization_barrier(jnp.sum(img_wide * img_wide, axis=-1))) * jnp.sqrt(lax.optimization_barrier(jnp.sum(img_pre * img_pre, axis=-1)))
    txt_norms = jnp.sqrt(lax.optimization_barrier(jnp.sum(txt_wide * txt_wide, axis=-1))) * jnp.sqrt(lax.optimization_barrier(jnp.sum(txt_pre * txt_pre, axis=-1)))
    return (img_proj_grad, txt_proj_grad, img_norms, txt_norms)
```

```python
import jax
import jax.numpy as jnp
from jax import lax
from jax.sharding import Mesh, PartitionSpec as P

EVERY = ("zlo", "core", "y", "zhi", "x")
SWAP = [(0, 1), (1, 0)]


def turned(value, axis, by):
    count = lax.axis_size(axis)
    return lax.ppermute(value, axis, [(i, (i + by) % count) for i in range(count)])


def spread(value, axis):
    count = lax.axis_size(axis)
    copies = jnp.broadcast_to(value[None], (count,) + value.shape)
    return lax.all_to_all(copies, axis, split_axis=0, concat_axis=0)


def on_device(
    picture_inputs,
    caption_inputs,
    picture_mapping,
    caption_mapping,
    similarity_multiplier,
    score_constant,
):
    own, width = picture_inputs.shape
    embed = picture_mapping.shape[1]
    share = picture_mapping.shape[0]
    first = lax.axis_index("core") == 0
    chips = lax.axis_size("zlo")
    n_y, n_zhi, n_x = lax.axis_size("y"), lax.axis_size("zhi"), lax.axis_size("x")
    mine = jnp.where(first, picture_inputs, caption_inputs)
    sent = jnp.where(first, caption_inputs, picture_inputs)
    chunk = jnp.concatenate([mine, lax.ppermute(sent, "core", SWAP)], axis=0)
    from_1, from_3 = turned(chunk, "zlo", 1), turned(chunk, "zlo", 3)
    from_2 = turned(chunk, "zlo", 2)
    piece = jnp.where(first, picture_mapping, caption_mapping)
    paired = jnp.concatenate([piece, lax.ppermute(piece, "zhi", SWAP)], axis=0)
    near = spread(paired, "y").reshape(n_y * n_zhi * share, embed)
    after = jnp.minimum(jnp.abs(from_1[0, 0]), 0) + jnp.minimum(jnp.abs(from_3[0, 0]), 0)
    gathered = spread(near + after, "x").reshape(width, embed)
    rows = jnp.concatenate([chunk, from_1, from_2, from_3], axis=0)
    at = jnp.arange(width, dtype=jnp.int32)
    owner, row = at // share, at % share
    at_half = (owner // n_x) % n_zhi
    at_half = jnp.where(lax.axis_index("zhi") == 0, at_half, 1 - at_half)
    place = (((owner % n_x) * n_y + owner // (n_x * n_zhi)) * n_zhi + at_half) * share + row
    order = (place[:, None] == at[None, :]).astype(jnp.bfloat16)
    mapping = jnp.dot(order, gathered, preferred_element_type=jnp.float32).astype(jnp.bfloat16)
    out = jnp.dot(rows, mapping, preferred_element_type=jnp.float32)
    radius = jnp.sqrt(jnp.sum(out * out, axis=-1, keepdims=True) + 1e-06)
    unit = out / radius
    half = unit.astype(jnp.bfloat16)
    partner = lax.ppermute(half, "core", SWAP)
    multiplier_amount = similarity_multiplier[0]
    logits = (
        multiplier_amount * jnp.dot(half, partner.T, preferred_element_type=jnp.float32)
        + score_constant[0]
    )
    ids = jnp.arange(rows.shape[0], dtype=jnp.int32)
    other_ids = ids + own - 2 * own * ((ids // own) % 2)
    sign = jnp.where(ids[:, None] == other_ids[None, :], 1.0, -1.0).astype(jnp.float32)
    weights = (-multiplier_amount * sign * jax.nn.sigmoid(-sign * logits)).astype(jnp.bfloat16)
    grad = jnp.dot(weights, partner, preferred_element_type=jnp.float32)
    pre = (grad - unit * jnp.sum(unit * grad, axis=-1, keepdims=True)) / radius
    columns = embed // chips
    part = lax.dynamic_slice_in_dim(pre, lax.axis_index("zlo") * columns, columns, axis=1)
    local = lax.dot_general(
        rows,
        part.astype(jnp.bfloat16),
        (((0,), (0,)), ((), ())),
        preferred_element_type=jnp.float32,
    )
    pieces = lax.all_to_all(
        local.astype(jnp.bfloat16).reshape(width // share, share, columns),
        ("y", "zhi", "x"),
        split_axis=0,
        concat_axis=0,
        tiled=True,
    )
    total = jnp.sum(pieces.astype(jnp.float32), axis=0)
    whole = spread(total, ("zlo", "core")).reshape(chips, 2, share, columns)
    whole = whole.transpose(1, 2, 0, 3).reshape(2, share, embed)
    wide = chunk.astype(jnp.float32)
    pre_chunk = pre[: 2 * own]
    norms = jnp.sqrt(jnp.sum(wide * wide, axis=-1)) * jnp.sqrt(
        jnp.sum(pre_chunk * pre_chunk, axis=-1)
    )
    own_norms = norms[:own]
    their_norms = lax.ppermute(norms[own:], "core", SWAP)
    img_norms = jnp.where(first, own_norms, their_norms)
    txt_norms = jnp.where(first, their_norms, own_norms)
    return (whole[0], whole[1], img_norms, txt_norms)


def solution(mesh):
    fine = Mesh(mesh.devices.reshape(4, 2, 8, 2, 4), EVERY)
    grp = ("y", "zhi", "x")
    in_specs = (P(EVERY, None), P(EVERY, None), P(grp, None), P(grp, None), P(), P())
    out_specs = (P(grp, None), P(grp, None), P(EVERY), P(EVERY))
    return jax.shard_map(
        on_device, mesh=fine, in_specs=in_specs, out_specs=out_specs, check_vma=False
    )
```

```python
import functools

import jax
import jax.numpy as jnp
from jax import lax
from jax.experimental import pallas as pl
from jax.experimental.pallas import tpu as pltpu
from jax.sharding import Mesh, PartitionSpec as P

EVERY = ("zlo", "core", "y", "zhi", "x")
GRP = ("y", "zhi", "x")
SWAP = [(0, 1), (1, 0)]
F32, BF16 = jnp.float32, jnp.bfloat16
VMEM = pl.BlockSpec(memory_space=pltpu.VMEM)
ANY = pl.BlockSpec(memory_space=pl.ANY)
SMEM = pl.BlockSpec(memory_space=pltpu.SMEM)
PARAMS = pltpu.CompilerParams(vmem_limit_bytes=40 * 1024 * 1024)


def passed_on(value, axis, by):
    count = lax.axis_size(axis)
    return lax.ppermute(value, axis, [(i, i + by) for i in range(count) if 0 <= i + by < count])


def spread(value, axis):
    count = lax.axis_size(axis)
    copies = jnp.broadcast_to(value[None], (count,) + value.shape)
    return lax.all_to_all(copies, axis, split_axis=0, concat_axis=0)


def copies_kernel(own_ref, other_ref, up_ref, down_ref, out_ref):
    share = own_ref.shape[0]
    for k in range(out_ref.shape[0]):
        out_ref[k, :share] = own_ref[...]
        out_ref[k, share:] = other_ref[...]


def spread_kernel(near_ref, up_ref, down_ref, out_ref):
    for k in range(out_ref.shape[0]):
        out_ref[k] = near_ref[...]


def embed_kernel(
    place, order_ref, gathered_ref, x0, up1, up2, up3, down1, down2, down3,
    half_ref, unit_ref, radius_ref, rows_ref, mapping,
):
    mapping[...] = jnp.dot(
        order_ref[...], gathered_ref[...], preferred_element_type=F32
    ).astype(BF16)
    blocks = ((x0, None), (up1, down3), (up2, down2), (up3, down1))
    for k, (low, high) in enumerate(blocks):
        rows = low.shape[0]
        at = pl.ds(k * rows, rows)
        block = low[...] if high is None else jnp.where(place[0] >= k, low[...], high[...])
        rows_ref[at, :] = block
        out = jnp.dot(block, mapping[...], preferred_element_type=F32)
        radius = jnp.sqrt(jnp.sum(out * out, axis=-1, keepdims=True) + 1e-06)
        unit = out / radius
        radius_ref[at, :] = radius
        unit_ref[at, :] = unit
        half_ref[at, :] = unit.astype(BF16)


def grad_kernel(
    own, scalars, place, half_ref, partner_ref, unit_ref, radius_ref, rows_ref,
    local_ref, norms_ref, pre_ref,
):
    multiplier, offset = scalars[0], scalars[1]
    columns = local_ref.shape[1]
    start = pl.multiple_of((3 * place[0]) // 2 * 128, 128)
    total = None
    rows = 2 * own
    for k in range(rows_ref.shape[0] // rows):
        at = pl.ds(k * rows, rows)
        logits = multiplier * lax.dot_general(
            half_ref[at, :], partner_ref[...], (((1,), (1,)), ((), ())), preferred_element_type=F32
        ) + offset
        i = lax.broadcasted_iota(jnp.int32, logits.shape, 0) + k * rows
        j = lax.broadcasted_iota(jnp.int32, logits.shape, 1)
        sign = jnp.where(j == jnp.where(i % rows < own, i + own, i - own), 1.0, -1.0)
        weights = (-multiplier * sign) * jax.nn.sigmoid(-sign * logits)
        grad = jnp.dot(weights.astype(BF16), partner_ref[...], preferred_element_type=F32)
        unit = unit_ref[at, :]
        pre = (grad - unit * jnp.sum(unit * grad, axis=-1, keepdims=True)) / radius_ref[at, :]
        pre_ref[...] = pre
        if k == 0:
            wide = rows_ref[at, :].astype(F32)
            norms_ref[...] = jnp.sqrt(jnp.sum(wide * wide, axis=-1, keepdims=True)) * jnp.sqrt(
                jnp.sum(pre * pre, axis=-1, keepdims=True)
            )
        part = lax.dot_general(
            rows_ref[at, :],
            pre_ref[:, pl.ds(start, 256)].astype(BF16),
            (((0,), (0,)), ((), ())),
            preferred_element_type=F32,
        )
        total = part if total is None else total + part
    odd = place[0] % 2 == 1
    local_ref[...] = jnp.where(odd, total[:, 256 - columns :], total[:, :columns]).astype(BF16)


def on_device(
    picture_inputs,
    caption_inputs,
    picture_mapping,
    caption_mapping,
    similarity_multiplier,
    score_constant,
):
    own, width = picture_inputs.shape
    share, embed = picture_mapping.shape
    first = lax.axis_index("core") == 0
    chips = lax.axis_size("zlo")
    n_y, n_zhi, n_x = (lax.axis_size(a) for a in GRP)
    piece = jnp.where(first, picture_mapping, caption_mapping)
    other = lax.ppermute(piece, "zhi", SWAP)
    mine = jnp.where(first, picture_inputs, caption_inputs)
    sent = jnp.where(first, caption_inputs, picture_inputs)
    chunk = jnp.concatenate([mine, lax.ppermute(sent, "core", SWAP)], axis=0)
    up, down = [chunk], [chunk]
    for _ in range(1, chips):
        up.append(passed_on(up[-1], "zlo", 1))
        down.append(passed_on(down[-1], "zlo", -1))
    at_chip = lax.axis_index("zlo").astype(jnp.int32).reshape(1)
    copies = pl.pallas_call(
        copies_kernel,
        out_shape=jax.ShapeDtypeStruct((n_y, n_zhi * share, embed), BF16),
        in_specs=[VMEM, VMEM, ANY, ANY],
        out_specs=VMEM,
        cost_estimate=pl.CostEstimate(flops=0, bytes_accessed=2**19, transcendentals=0),
    )(piece, other, up[1], down[1])
    near = lax.all_to_all(copies, "y", split_axis=0, concat_axis=0)
    near = near.reshape(n_y * n_zhi * share, embed)
    copies = pl.pallas_call(
        spread_kernel,
        out_shape=jax.ShapeDtypeStruct((n_x,) + near.shape, BF16),
        in_specs=[VMEM, ANY, ANY],
        out_specs=VMEM,
        cost_estimate=pl.CostEstimate(flops=0, bytes_accessed=2**21, transcendentals=0),
    )(near, up[2], down[2])
    gathered = lax.all_to_all(copies, "x", split_axis=0, concat_axis=0).reshape(width, embed)
    at = jnp.arange(width, dtype=jnp.int32)
    owner, row = at // share, at % share
    at_half = (owner // n_x) % n_zhi
    at_half = jnp.where(lax.axis_index("zhi") == 0, at_half, 1 - at_half)
    from_row = (((owner % n_x) * n_y + owner // (n_x * n_zhi)) * n_zhi + at_half) * share + row
    order = (from_row[:, None] == at[None, :]).astype(BF16)
    rows = chips * chunk.shape[0]
    half, unit, radius, set_rows = pl.pallas_call(
        embed_kernel,
        out_shape=(
            jax.ShapeDtypeStruct((rows, embed), BF16),
            jax.ShapeDtypeStruct((rows, embed), F32),
            jax.ShapeDtypeStruct((rows, 1), F32),
            jax.ShapeDtypeStruct((rows, width), BF16),
        ),
        in_specs=[SMEM] + [VMEM] * 9,
        out_specs=(VMEM,) * 4,
        scratch_shapes=[pltpu.VMEM((width, embed), BF16)],
        compiler_params=PARAMS,
        cost_estimate=pl.CostEstimate(
            flops=2 * (rows + width) * width * embed, bytes_accessed=8 * 2**20, transcendentals=0
        ),
    )(at_chip, order, gathered, *up, *down[1:])
    partner = lax.ppermute(half, "core", SWAP)
    columns = embed // chips
    local, norms = pl.pallas_call(
        functools.partial(grad_kernel, own),
        out_shape=(
            jax.ShapeDtypeStruct((width, columns), BF16),
            jax.ShapeDtypeStruct((2 * own, 1), F32),
        ),
        in_specs=[SMEM] * 2 + [VMEM] * 5,
        out_specs=(VMEM,) * 2,
        scratch_shapes=[pltpu.VMEM((2 * own, embed), F32)],
        compiler_params=PARAMS,
        cost_estimate=pl.CostEstimate(
            flops=4 * rows * rows * embed, bytes_accessed=8 * 2**20, transcendentals=rows * rows
        ),
    )(
        jnp.concatenate([similarity_multiplier, score_constant]),
        at_chip,
        half,
        partner,
        unit,
        radius,
        set_rows,
    )
    pieces = lax.all_to_all(
        local.reshape(width // share, share, columns), GRP, split_axis=0, concat_axis=0, tiled=True
    )
    total = jnp.sum(pieces.astype(F32), axis=0)
    whole = spread(total, ("zlo", "core")).reshape(chips, 2, share, columns)
    whole = whole.transpose(1, 2, 0, 3).reshape(2, share, embed)
    norms = norms.reshape(2 * own)
    own_norms = norms[:own]
    their_norms = lax.ppermute(norms[own:], "core", SWAP)
    img_norms = jnp.where(first, own_norms, their_norms)
    txt_norms = jnp.where(first, their_norms, own_norms)
    return (whole[0], whole[1], img_norms, txt_norms)


def build(fine):
    in_specs = (P(EVERY, None), P(EVERY, None), P(GRP, None), P(GRP, None), P(), P())
    out_specs = (P(GRP, None), P(GRP, None), P(EVERY), P(EVERY))
    return jax.shard_map(
        on_device, mesh=fine, in_specs=in_specs, out_specs=out_specs, check_vma=False
    )


def solution(mesh):
    return build(Mesh(mesh.devices.reshape(4, 2, 8, 2, 4), EVERY))
```

```python
import functools

import jax
import jax.numpy as jnp
from jax import lax
from jax.experimental import pallas as pl
from jax.experimental.pallas import tpu as pltpu
from jax.sharding import Mesh, PartitionSpec as P

EVERY = ("zlo", "core", "y", "zhi", "x")
GRP = ("y", "zhi", "x")
SWAP = [(0, 1), (1, 0)]
F32, BF16 = jnp.float32, jnp.bfloat16
VMEM = pl.BlockSpec(memory_space=pltpu.VMEM)
SMEM = pl.BlockSpec(memory_space=pltpu.SMEM)
PARAMS = pltpu.CompilerParams(vmem_limit_bytes=40 * 1024 * 1024)


def spread(value, axis):
    count = lax.axis_size(axis)
    copies = jnp.broadcast_to(value[None], (count,) + value.shape)
    return lax.all_to_all(copies, axis, split_axis=0, concat_axis=0)


def copies_kernel(own_ref, other_ref, out_ref):
    share = own_ref.shape[0]
    for k in range(out_ref.shape[0]):
        out_ref[k, :share] = own_ref[...]
        out_ref[k, share:] = other_ref[...]


def spread_kernel(near_ref, out_ref):
    for k in range(out_ref.shape[0]):
        out_ref[k] = near_ref[...]


def embed_kernel(order_ref, gathered_ref, rows_ref, half_ref, unit_ref, radius_ref, mapping):
    mapping[...] = jnp.dot(
        order_ref[...], gathered_ref[...], preferred_element_type=F32
    ).astype(BF16)
    block = 256
    for k in range(rows_ref.shape[0] // block):
        at = pl.ds(k * block, block)
        out = jnp.dot(rows_ref[at, :], mapping[...], preferred_element_type=F32)
        radius = jnp.sqrt(jnp.sum(out * out, axis=-1, keepdims=True) + 1e-06)
        unit = out / radius
        radius_ref[at, :] = radius
        unit_ref[at, :] = unit
        half_ref[at, :] = unit.astype(BF16)


def grad_kernel(
    own, scalars, place, half_ref, partner_ref, unit_ref, radius_ref, rows_ref,
    local_ref, norms_ref, pre_ref,
):
    multiplier, offset = scalars[0], scalars[1]
    columns = local_ref.shape[1]
    start = pl.multiple_of((3 * place[0]) // 2 * 128, 128)
    total = None
    rows = 2 * own
    for k in range(rows_ref.shape[0] // rows):
        at = pl.ds(k * rows, rows)
        logits = multiplier * lax.dot_general(
            half_ref[at, :], partner_ref[...], (((1,), (1,)), ((), ())), preferred_element_type=F32
        ) + offset
        i = lax.broadcasted_iota(jnp.int32, logits.shape, 0) + k * rows
        j = lax.broadcasted_iota(jnp.int32, logits.shape, 1)
        sign = jnp.where(j == jnp.where(i % rows < own, i + own, i - own), 1.0, -1.0)
        weights = (-multiplier * sign) * jax.nn.sigmoid(-sign * logits)
        grad = jnp.dot(weights.astype(BF16), partner_ref[...], preferred_element_type=F32)
        unit = unit_ref[at, :]
        pre = (grad - unit * jnp.sum(unit * grad, axis=-1, keepdims=True)) / radius_ref[at, :]
        pre_ref[...] = pre

        @pl.when(place[0] == k)
        def _():
            wide = rows_ref[at, :].astype(F32)
            norms_ref[...] = jnp.sqrt(jnp.sum(wide * wide, axis=-1, keepdims=True)) * jnp.sqrt(
                jnp.sum(pre * pre, axis=-1, keepdims=True)
            )

        part = lax.dot_general(
            rows_ref[at, :],
            pre_ref[:, pl.ds(start, 256)].astype(BF16),
            (((0,), (0,)), ((), ())),
            preferred_element_type=F32,
        )
        total = part if total is None else total + part
    odd = place[0] % 2 == 1
    local_ref[...] = jnp.where(odd, total[:, 256 - columns :], total[:, :columns]).astype(BF16)


def on_device(
    picture_inputs,
    caption_inputs,
    picture_mapping,
    caption_mapping,
    similarity_multiplier,
    score_constant,
):
    own, width = picture_inputs.shape
    share, embed = picture_mapping.shape
    first = lax.axis_index("core") == 0
    chips = lax.axis_size("zlo")
    n_y, n_zhi, n_x = (lax.axis_size(a) for a in GRP)
    piece = jnp.where(first, picture_mapping, caption_mapping)
    other = lax.ppermute(piece, "zhi", SWAP)
    mine = jnp.where(first, picture_inputs, caption_inputs)
    sent = jnp.where(first, caption_inputs, picture_inputs)
    chunk = jnp.concatenate([mine, lax.ppermute(sent, "core", SWAP)], axis=0)
    set_rows = lax.all_gather(chunk, "zlo", axis=0, tiled=True)
    at_chip = lax.axis_index("zlo").astype(jnp.int32).reshape(1)
    copies = pl.pallas_call(
        copies_kernel,
        out_shape=jax.ShapeDtypeStruct((n_y, n_zhi * share, embed), BF16),
        in_specs=[VMEM] * 2,
        out_specs=VMEM,
        cost_estimate=pl.CostEstimate(flops=0, bytes_accessed=2**19, transcendentals=0),
    )(piece, other)
    near = lax.all_to_all(copies, "y", split_axis=0, concat_axis=0)
    near = near.reshape(n_y * n_zhi * share, embed)
    copies = pl.pallas_call(
        spread_kernel,
        out_shape=jax.ShapeDtypeStruct((n_x,) + near.shape, BF16),
        in_specs=[VMEM],
        out_specs=VMEM,
        cost_estimate=pl.CostEstimate(flops=0, bytes_accessed=2**21, transcendentals=0),
    )(near)
    gathered = lax.all_to_all(copies, "x", split_axis=0, concat_axis=0).reshape(width, embed)
    at = jnp.arange(width, dtype=jnp.int32)
    owner, row = at // share, at % share
    at_half = (owner // n_x) % n_zhi
    at_half = jnp.where(lax.axis_index("zhi") == 0, at_half, 1 - at_half)
    from_row = (((owner % n_x) * n_y + owner // (n_x * n_zhi)) * n_zhi + at_half) * share + row
    order = (from_row[:, None] == at[None, :]).astype(BF16)
    rows = chips * chunk.shape[0]
    half, unit, radius = pl.pallas_call(
        embed_kernel,
        out_shape=(
            jax.ShapeDtypeStruct((rows, embed), BF16),
            jax.ShapeDtypeStruct((rows, embed), F32),
            jax.ShapeDtypeStruct((rows, 1), F32),
        ),
        in_specs=[VMEM] * 3,
        out_specs=(VMEM,) * 3,
        scratch_shapes=[pltpu.VMEM((width, embed), BF16)],
        compiler_params=PARAMS,
        cost_estimate=pl.CostEstimate(
            flops=2 * (rows + width) * width * embed, bytes_accessed=8 * 2**20, transcendentals=0
        ),
    )(order, gathered, set_rows)
    partner = lax.ppermute(half, "core", SWAP)
    columns = embed // chips
    local, norms = pl.pallas_call(
        functools.partial(grad_kernel, own),
        out_shape=(
            jax.ShapeDtypeStruct((width, columns), BF16),
            jax.ShapeDtypeStruct((2 * own, 1), F32),
        ),
        in_specs=[SMEM] * 2 + [VMEM] * 5,
        out_specs=(VMEM,) * 2,
        scratch_shapes=[pltpu.VMEM((2 * own, embed), F32)],
        compiler_params=PARAMS,
        cost_estimate=pl.CostEstimate(
            flops=4 * rows * rows * embed, bytes_accessed=8 * 2**20, transcendentals=rows * rows
        ),
    )(
        jnp.concatenate([similarity_multiplier, score_constant]),
        at_chip,
        half,
        partner,
        unit,
        radius,
        set_rows,
    )
    pieces = lax.all_to_all(
        local.reshape(width // share, share, columns), GRP, split_axis=0, concat_axis=0, tiled=True
    )
    total = jnp.sum(pieces.astype(F32), axis=0)
    whole = spread(total, ("zlo", "core")).reshape(chips, 2, share, columns)
    whole = whole.transpose(1, 2, 0, 3).reshape(2, share, embed)
    norms = norms.reshape(2 * own)
    own_norms = norms[:own]
    their_norms = lax.ppermute(norms[own:], "core", SWAP)
    img_norms = jnp.where(first, own_norms, their_norms)
    txt_norms = jnp.where(first, their_norms, own_norms)
    return (whole[0], whole[1], img_norms, txt_norms)


def build(fine):
    in_specs = (P(EVERY, None), P(EVERY, None), P(GRP, None), P(GRP, None), P(), P())
    out_specs = (P(GRP, None), P(GRP, None), P(EVERY), P(EVERY))
    return jax.shard_map(
        on_device, mesh=fine, in_specs=in_specs, out_specs=out_specs, check_vma=False
    )


def solution(mesh):
    return build(Mesh(mesh.devices.reshape(4, 2, 8, 2, 4), EVERY))
```

```python
import functools

import jax
import jax.numpy as jnp
from jax import lax
from jax.experimental import pallas as pl
from jax.experimental.pallas import tpu as pltpu
from jax.sharding import Mesh, PartitionSpec as P

EVERY = ("zlo", "core", "y", "zhi", "x")
GRP = ("y", "zhi", "x")
SWAP = [(0, 1), (1, 0)]
F32, BF16 = jnp.float32, jnp.bfloat16
VMEM = pl.BlockSpec(memory_space=pltpu.VMEM)
STACK = 10**10
SMEM = pl.BlockSpec(memory_space=pltpu.SMEM)
PARAMS = pltpu.CompilerParams(vmem_limit_bytes=40 * 1024 * 1024)


def turned(value, axis, by):
    count = lax.axis_size(axis)
    return lax.ppermute(value, axis, [(i, (i + by) % count) for i in range(count)])


def spread(value, axis):
    count = lax.axis_size(axis)
    copies = jnp.broadcast_to(value[None], (count,) + value.shape)
    return lax.all_to_all(copies, axis, split_axis=0, concat_axis=0)


def copies_kernel(own_ref, other_ref, out_ref):
    share = own_ref.shape[0]
    for k in range(out_ref.shape[0]):
        out_ref[k, :share] = own_ref[...]
        out_ref[k, share:] = other_ref[...]


def spread_kernel(near_ref, out_ref):
    for k in range(out_ref.shape[0]):
        out_ref[k] = near_ref[...]


def stack_kernel(x0, x1, x2, x3, rows_ref):
    rows = x0.shape[0]
    for k, x in enumerate((x0, x1, x2, x3)):
        rows_ref[pl.ds(k * rows, rows), :] = x[...]


def embed_kernel(order_ref, gathered_ref, rows_ref, half_ref, unit_ref, radius_ref, mapping):
    mapping[...] = jnp.dot(
        order_ref[...], gathered_ref[...], preferred_element_type=F32
    ).astype(BF16)
    block = 256
    for k in range(rows_ref.shape[0] // block):
        at = pl.ds(k * block, block)
        out = jnp.dot(rows_ref[at, :], mapping[...], preferred_element_type=F32)
        radius = jnp.sqrt(jnp.sum(out * out, axis=-1, keepdims=True) + 1e-06)
        unit = out / radius
        radius_ref[at, :] = radius
        unit_ref[at, :] = unit
        half_ref[at, :] = unit.astype(BF16)


def grad_kernel(
    own, scalars, place, half_ref, partner_ref, unit_ref, radius_ref, rows_ref,
    local_ref, norms_ref, pre_ref,
):
    multiplier, offset = scalars[0], scalars[1]
    columns = local_ref.shape[1]
    start = pl.multiple_of((3 * place[0]) // 2 * 128, 128)
    total = None
    rows = 2 * own
    for k in range(rows_ref.shape[0] // rows):
        at = pl.ds(k * rows, rows)
        logits = multiplier * lax.dot_general(
            half_ref[at, :], partner_ref[...], (((1,), (1,)), ((), ())), preferred_element_type=F32
        ) + offset
        i = lax.broadcasted_iota(jnp.int32, logits.shape, 0) + k * rows
        j = lax.broadcasted_iota(jnp.int32, logits.shape, 1)
        sign = jnp.where(j == jnp.where(i % rows < own, i + own, i - own), 1.0, -1.0)
        weights = (-multiplier * sign) * jax.nn.sigmoid(-sign * logits)
        grad = jnp.dot(weights.astype(BF16), partner_ref[...], preferred_element_type=F32)
        unit = unit_ref[at, :]
        pre = (grad - unit * jnp.sum(unit * grad, axis=-1, keepdims=True)) / radius_ref[at, :]
        pre_ref[...] = pre
        if k == 0:
            wide = rows_ref[at, :].astype(F32)
            norms_ref[...] = jnp.sqrt(jnp.sum(wide * wide, axis=-1, keepdims=True)) * jnp.sqrt(
                jnp.sum(pre * pre, axis=-1, keepdims=True)
            )
        part = lax.dot_general(
            rows_ref[at, :],
            pre_ref[:, pl.ds(start, 256)].astype(BF16),
            (((0,), (0,)), ((), ())),
            preferred_element_type=F32,
        )
        total = part if total is None else total + part
    odd = place[0] % 2 == 1
    local_ref[...] = jnp.where(odd, total[:, 256 - columns :], total[:, :columns]).astype(BF16)


def on_device(
    picture_inputs,
    caption_inputs,
    picture_mapping,
    caption_mapping,
    similarity_multiplier,
    score_constant,
):
    own, width = picture_inputs.shape
    share, embed = picture_mapping.shape
    first = lax.axis_index("core") == 0
    chips = lax.axis_size("zlo")
    n_y, n_zhi, n_x = (lax.axis_size(a) for a in GRP)
    piece = jnp.where(first, picture_mapping, caption_mapping)
    other = lax.ppermute(piece, "zhi", SWAP)
    mine = jnp.where(first, picture_inputs, caption_inputs)
    sent = jnp.where(first, caption_inputs, picture_inputs)
    chunk = jnp.concatenate([mine, lax.ppermute(sent, "core", SWAP)], axis=0)
    chunks = [chunk] + [turned(chunk, "zlo", k) for k in range(1, chips)]
    set_rows = pl.pallas_call(
        stack_kernel,
        out_shape=jax.ShapeDtypeStruct((chips * 2 * own, width), BF16),
        in_specs=[VMEM] * 4,
        out_specs=VMEM,
        cost_estimate=pl.CostEstimate(flops=STACK, bytes_accessed=2**21, transcendentals=0),
    )(*chunks)
    at_chip = lax.axis_index("zlo").astype(jnp.int32).reshape(1)
    copies = pl.pallas_call(
        copies_kernel,
        out_shape=jax.ShapeDtypeStruct((n_y, n_zhi * share, embed), BF16),
        in_specs=[VMEM] * 2,
        out_specs=VMEM,
        cost_estimate=pl.CostEstimate(flops=0, bytes_accessed=2**19, transcendentals=0),
    )(piece, other)
    near = lax.all_to_all(copies, "y", split_axis=0, concat_axis=0)
    near = near.reshape(n_y * n_zhi * share, embed)
    copies = pl.pallas_call(
        spread_kernel,
        out_shape=jax.ShapeDtypeStruct((n_x,) + near.shape, BF16),
        in_specs=[VMEM],
        out_specs=VMEM,
        cost_estimate=pl.CostEstimate(flops=0, bytes_accessed=2**21, transcendentals=0),
    )(near)
    gathered = lax.all_to_all(copies, "x", split_axis=0, concat_axis=0).reshape(width, embed)
    at = jnp.arange(width, dtype=jnp.int32)
    owner, row = at // share, at % share
    at_half = (owner // n_x) % n_zhi
    at_half = jnp.where(lax.axis_index("zhi") == 0, at_half, 1 - at_half)
    from_row = (((owner % n_x) * n_y + owner // (n_x * n_zhi)) * n_zhi + at_half) * share + row
    order = (from_row[:, None] == at[None, :]).astype(BF16)
    rows = chips * chunk.shape[0]
    half, unit, radius = pl.pallas_call(
        embed_kernel,
        out_shape=(
            jax.ShapeDtypeStruct((rows, embed), BF16),
            jax.ShapeDtypeStruct((rows, embed), F32),
            jax.ShapeDtypeStruct((rows, 1), F32),
        ),
        in_specs=[VMEM] * 3,
        out_specs=(VMEM,) * 3,
        scratch_shapes=[pltpu.VMEM((width, embed), BF16)],
        compiler_params=PARAMS,
        cost_estimate=pl.CostEstimate(
            flops=2 * (rows + width) * width * embed, bytes_accessed=8 * 2**20, transcendentals=0
        ),
    )(order, gathered, set_rows)
    partner = lax.ppermute(half, "core", SWAP)
    columns = embed // chips
    local, norms = pl.pallas_call(
        functools.partial(grad_kernel, own),
        out_shape=(
            jax.ShapeDtypeStruct((width, columns), BF16),
            jax.ShapeDtypeStruct((2 * own, 1), F32),
        ),
        in_specs=[SMEM] * 2 + [VMEM] * 5,
        out_specs=(VMEM,) * 2,
        scratch_shapes=[pltpu.VMEM((2 * own, embed), F32)],
        compiler_params=PARAMS,
        cost_estimate=pl.CostEstimate(
            flops=4 * rows * rows * embed, bytes_accessed=8 * 2**20, transcendentals=rows * rows
        ),
    )(
        jnp.concatenate([similarity_multiplier, score_constant]),
        at_chip,
        half,
        partner,
        unit,
        radius,
        set_rows,
    )
    pieces = lax.all_to_all(
        local.reshape(width // share, share, columns), GRP, split_axis=0, concat_axis=0, tiled=True
    )
    total = jnp.sum(pieces.astype(F32), axis=0)
    whole = spread(total, ("zlo", "core")).reshape(chips, 2, share, columns)
    whole = whole.transpose(1, 2, 0, 3).reshape(2, share, embed)
    norms = norms.reshape(2 * own)
    own_norms = norms[:own]
    their_norms = lax.ppermute(norms[own:], "core", SWAP)
    img_norms = jnp.where(first, own_norms, their_norms)
    txt_norms = jnp.where(first, their_norms, own_norms)
    return (whole[0], whole[1], img_norms, txt_norms)


def build(fine):
    in_specs = (P(EVERY, None), P(EVERY, None), P(GRP, None), P(GRP, None), P(), P())
    out_specs = (P(GRP, None), P(GRP, None), P(EVERY), P(EVERY))
    return jax.shard_map(
        on_device, mesh=fine, in_specs=in_specs, out_specs=out_specs, check_vma=False
    )


def solution(mesh):
    return build(Mesh(mesh.devices.reshape(4, 2, 8, 2, 4), EVERY))
```

```python
import functools

import jax
import jax.numpy as jnp
from jax import lax
from jax.experimental import pallas as pl
from jax.experimental.pallas import tpu as pltpu
from jax.sharding import Mesh, PartitionSpec as P

EVERY = ("zlo", "core", "y", "zhi", "x")
GRP = ("y", "zhi", "x")
SWAP = [(0, 1), (1, 0)]
F32, BF16 = jnp.float32, jnp.bfloat16
VMEM = pl.BlockSpec(memory_space=pltpu.VMEM)
STACK = 10**10
SMEM = pl.BlockSpec(memory_space=pltpu.SMEM)
PARAMS = pltpu.CompilerParams(vmem_limit_bytes=24 * 1024 * 1024)


def turned(value, axis, by):
    count = lax.axis_size(axis)
    return lax.ppermute(value, axis, [(i, (i + by) % count) for i in range(count)])


def spread(value, axis):
    count = lax.axis_size(axis)
    copies = jnp.broadcast_to(value[None], (count,) + value.shape)
    return lax.all_to_all(copies, axis, split_axis=0, concat_axis=0)


def stack_kernel(x0, x1, x2, x3, rows_ref):
    rows = x0.shape[0]
    for k, x in enumerate((x0, x1, x2, x3)):
        rows_ref[pl.ds(k * rows, rows), :] = x[...]


def embed_kernel(order_ref, gathered_ref, rows_ref, half_ref, unit_ref, radius_ref, mapping):
    mapping[...] = jnp.dot(
        order_ref[...], gathered_ref[...], preferred_element_type=F32
    ).astype(BF16)
    block = 256
    for k in range(rows_ref.shape[0] // block):
        at = pl.ds(k * block, block)
        out = jnp.dot(rows_ref[at, :], mapping[...], preferred_element_type=F32)
        radius = jnp.sqrt(jnp.sum(out * out, axis=-1, keepdims=True) + 1e-06)
        unit = out / radius
        radius_ref[at, :] = radius
        unit_ref[at, :] = unit
        half_ref[at, :] = unit.astype(BF16)


def grad_kernel(
    own, scalars, place, half_ref, partner_ref, unit_ref, radius_ref, rows_ref,
    local_ref, norms_ref, pre_ref,
):
    multiplier, offset = scalars[0], scalars[1]
    owners, share, columns = local_ref.shape
    start = pl.multiple_of((3 * place[0]) // 2 * 128, 128)
    total = None
    rows = 2 * own
    for k in range(rows_ref.shape[0] // rows):
        at = pl.ds(k * rows, rows)
        logits = multiplier * lax.dot_general(
            half_ref[at, :], partner_ref[...], (((1,), (1,)), ((), ())), preferred_element_type=F32
        ) + offset
        i = lax.broadcasted_iota(jnp.int32, logits.shape, 0) + k * rows
        j = lax.broadcasted_iota(jnp.int32, logits.shape, 1)
        sign = jnp.where(j == jnp.where(i % rows < own, i + own, i - own), 1.0, -1.0)
        weights = (-multiplier * sign) * jax.nn.sigmoid(-sign * logits)
        grad = jnp.dot(weights.astype(BF16), partner_ref[...], preferred_element_type=F32)
        unit = unit_ref[at, :]
        pre = (grad - unit * jnp.sum(unit * grad, axis=-1, keepdims=True)) / radius_ref[at, :]
        pre_ref[...] = pre
        if k == 0:
            wide = rows_ref[at, :].astype(F32)
            norms_ref[...] = jnp.sqrt(jnp.sum(wide * wide, axis=-1, keepdims=True)) * jnp.sqrt(
                jnp.sum(pre * pre, axis=-1, keepdims=True)
            )
        part = lax.dot_general(
            rows_ref[at, :],
            pre_ref[:, pl.ds(start, 256)].astype(BF16),
            (((0,), (0,)), ((), ())),
            preferred_element_type=F32,
        )
        total = part if total is None else total + part
    odd = place[0] % 2 == 1
    total = jnp.where(odd, total[:, 256 - columns :], total[:, :columns])
    for k in range(owners):
        local_ref[k] = total[k * share : (k + 1) * share].astype(BF16)


def sum_kernel(pieces_ref, out_ref):
    total = jnp.sum(pieces_ref[...].astype(F32), axis=0)
    for k in range(out_ref.shape[0]):
        out_ref[k] = total


def join_kernel(parts_ref, img_ref, txt_ref):
    for core, ref in enumerate((img_ref, txt_ref)):
        parts = [parts_ref[k] for k in range(core, parts_ref.shape[0], 2)]
        ref[...] = jnp.concatenate(parts, axis=1)


def on_device(
    picture_inputs,
    caption_inputs,
    picture_mapping,
    caption_mapping,
    similarity_multiplier,
    score_constant,
):
    own, width = picture_inputs.shape
    share, embed = picture_mapping.shape
    first = lax.axis_index("core") == 0
    chips = lax.axis_size("zlo")
    n_y, n_zhi, n_x = (lax.axis_size(a) for a in GRP)
    piece = jnp.where(first, picture_mapping, caption_mapping)
    mine = jnp.where(first, picture_inputs, caption_inputs)
    sent = jnp.where(first, caption_inputs, picture_inputs)
    chunk = jnp.concatenate([mine, lax.ppermute(sent, "core", SWAP)], axis=0)
    chunks = [chunk] + [turned(chunk, "zlo", k) for k in range(1, chips)]
    set_rows = pl.pallas_call(
        stack_kernel,
        out_shape=jax.ShapeDtypeStruct((chips * 2 * own, width), BF16),
        in_specs=[VMEM] * 4,
        out_specs=VMEM,
        cost_estimate=pl.CostEstimate(flops=STACK, bytes_accessed=2**21, transcendentals=0),
    )(*chunks)
    at_chip = lax.axis_index("zlo").astype(jnp.int32).reshape(1)
    near = spread(piece, ("y", "zhi")).reshape(n_y * n_zhi * share, embed)
    gathered = spread(near, "x").reshape(width, embed)
    at = jnp.arange(width, dtype=jnp.int32)
    owner, row = at // share, at % share
    from_row = ((owner % n_x) * (n_y * n_zhi) + owner // n_x) * share + row
    order = (from_row[:, None] == at[None, :]).astype(BF16)
    rows = chips * chunk.shape[0]
    half, unit, radius = pl.pallas_call(
        embed_kernel,
        out_shape=(
            jax.ShapeDtypeStruct((rows, embed), BF16),
            jax.ShapeDtypeStruct((rows, embed), F32),
            jax.ShapeDtypeStruct((rows, 1), F32),
        ),
        in_specs=[VMEM] * 3,
        out_specs=(VMEM,) * 3,
        scratch_shapes=[pltpu.VMEM((width, embed), BF16)],
        compiler_params=PARAMS,
        cost_estimate=pl.CostEstimate(
            flops=2 * (rows + width) * width * embed, bytes_accessed=8 * 2**20, transcendentals=0
        ),
    )(order, gathered, set_rows)
    partner = lax.ppermute(half, "core", SWAP)
    columns = embed // chips
    local, norms = pl.pallas_call(
        functools.partial(grad_kernel, own),
        out_shape=(
            jax.ShapeDtypeStruct((width // share, share, columns), BF16),
            jax.ShapeDtypeStruct((2 * own, 1), F32),
        ),
        in_specs=[SMEM] * 2 + [VMEM] * 5,
        out_specs=(VMEM,) * 2,
        scratch_shapes=[pltpu.VMEM((2 * own, embed), F32)],
        compiler_params=PARAMS,
        cost_estimate=pl.CostEstimate(
            flops=4 * rows * rows * embed, bytes_accessed=8 * 2**20, transcendentals=rows * rows
        ),
    )(
        jnp.concatenate([similarity_multiplier, score_constant]),
        at_chip,
        half,
        partner,
        unit,
        radius,
        set_rows,
    )
    pieces = lax.all_to_all(local, GRP, split_axis=0, concat_axis=0, tiled=True)
    totals = pl.pallas_call(
        sum_kernel,
        out_shape=jax.ShapeDtypeStruct((2 * chips, share, columns), F32),
        in_specs=[VMEM],
        out_specs=VMEM,
    )(pieces)
    parts = lax.all_to_all(totals, ("zlo", "core"), split_axis=0, concat_axis=0)
    img_proj_grad, txt_proj_grad = pl.pallas_call(
        join_kernel,
        out_shape=(jax.ShapeDtypeStruct((share, embed), F32),) * 2,
        in_specs=[VMEM],
        out_specs=(VMEM,) * 2,
    )(parts)
    norms = norms.reshape(2 * own)
    own_norms = norms[:own]
    their_norms = lax.ppermute(norms[own:], "core", SWAP)
    img_norms = jnp.where(first, own_norms, their_norms)
    txt_norms = jnp.where(first, their_norms, own_norms)
    return (img_proj_grad, txt_proj_grad, img_norms, txt_norms)


def build(fine):
    in_specs = (P(EVERY, None), P(EVERY, None), P(GRP, None), P(GRP, None), P(), P())
    out_specs = (P(GRP, None), P(GRP, None), P(EVERY), P(EVERY))
    return jax.shard_map(
        on_device, mesh=fine, in_specs=in_specs, out_specs=out_specs, check_vma=False
    )


def solution(mesh):
    return build(Mesh(mesh.devices.reshape(4, 2, 8, 2, 4), EVERY))
```

```python
import functools

import jax
import jax.numpy as jnp
from jax import lax
from jax.experimental import pallas as pl
from jax.experimental.pallas import tpu as pltpu
from jax.sharding import Mesh, PartitionSpec as P

EVERY = ("zlo", "core", "y", "zhi", "x")
GRP = ("y", "zhi", "x")
ARRIVED = 3 * 10**9
SWAP = [(0, 1), (1, 0)]
F32, BF16 = jnp.float32, jnp.bfloat16
VMEM = pl.BlockSpec(memory_space=pltpu.VMEM)
ANY = pl.BlockSpec(memory_space=pl.ANY)
SMEM = pl.BlockSpec(memory_space=pltpu.SMEM)
PARAMS = pltpu.CompilerParams(vmem_limit_bytes=40 * 1024 * 1024)


def passed_on(value, axis, by):
    count = lax.axis_size(axis)
    return lax.ppermute(value, axis, [(i, i + by) for i in range(count) if 0 <= i + by < count])


def spread(value, axis):
    count = lax.axis_size(axis)
    copies = jnp.broadcast_to(value[None], (count,) + value.shape)
    return lax.all_to_all(copies, axis, split_axis=0, concat_axis=0)


def copies_kernel(own_ref, other_ref, out_ref):
    share = own_ref.shape[0]
    for k in range(out_ref.shape[0]):
        out_ref[k, :share] = own_ref[...]
        out_ref[k, share:] = other_ref[...]


def arrived_kernel(up_ref, down_ref, out_ref):
    out_ref[...] = jnp.zeros_like(out_ref)


def embed_kernel(
    place, arrived_ref, order_ref, gathered_ref, x0, up1, up2, up3, down1, down2, down3,
    half_ref, unit_ref, radius_ref, rows_ref, mapping,
):
    mapping[...] = jnp.dot(
        order_ref[...], gathered_ref[...], preferred_element_type=F32
    ).astype(BF16)
    blocks = ((x0, None), (up1, down3), (up2, down2), (up3, down1))
    for k, (low, high) in enumerate(blocks):
        rows = low.shape[0]
        at = pl.ds(k * rows, rows)
        block = low[...] if high is None else jnp.where(place[0] >= k, low[...], high[...])
        rows_ref[at, :] = block
        out = jnp.dot(block, mapping[...], preferred_element_type=F32)
        radius = jnp.sqrt(jnp.sum(out * out, axis=-1, keepdims=True) + 1e-06)
        unit = out / radius
        radius_ref[at, :] = radius
        unit_ref[at, :] = unit
        half_ref[at, :] = unit.astype(BF16)


def grad_kernel(
    own, scalars, place, half_ref, partner_ref, unit_ref, radius_ref, rows_ref,
    local_ref, norms_ref, pre_ref,
):
    multiplier, offset = scalars[0], scalars[1]
    columns = local_ref.shape[1]
    start = pl.multiple_of((3 * place[0]) // 2 * 128, 128)
    total = None
    rows = 2 * own
    for k in range(rows_ref.shape[0] // rows):
        at = pl.ds(k * rows, rows)
        logits = multiplier * lax.dot_general(
            half_ref[at, :], partner_ref[...], (((1,), (1,)), ((), ())), preferred_element_type=F32
        ) + offset
        i = lax.broadcasted_iota(jnp.int32, logits.shape, 0) + k * rows
        j = lax.broadcasted_iota(jnp.int32, logits.shape, 1)
        sign = jnp.where(j == jnp.where(i % rows < own, i + own, i - own), 1.0, -1.0)
        weights = (-multiplier * sign) * jax.nn.sigmoid(-sign * logits)
        grad = jnp.dot(weights.astype(BF16), partner_ref[...], preferred_element_type=F32)
        unit = unit_ref[at, :]
        pre = (grad - unit * jnp.sum(unit * grad, axis=-1, keepdims=True)) / radius_ref[at, :]
        pre_ref[...] = pre
        if k == 0:
            wide = rows_ref[at, :].astype(F32)
            norms_ref[...] = jnp.sqrt(jnp.sum(wide * wide, axis=-1, keepdims=True)) * jnp.sqrt(
                jnp.sum(pre * pre, axis=-1, keepdims=True)
            )
        part = lax.dot_general(
            rows_ref[at, :],
            pre_ref[:, pl.ds(start, 256)].astype(BF16),
            (((0,), (0,)), ((), ())),
            preferred_element_type=F32,
        )
        total = part if total is None else total + part
    odd = place[0] % 2 == 1
    local_ref[...] = jnp.where(odd, total[:, 256 - columns :], total[:, :columns]).astype(BF16)


def on_device(
    picture_inputs,
    caption_inputs,
    picture_mapping,
    caption_mapping,
    similarity_multiplier,
    score_constant,
):
    own, width = picture_inputs.shape
    share, embed = picture_mapping.shape
    first = lax.axis_index("core") == 0
    chips = lax.axis_size("zlo")
    n_y, n_zhi, n_x = (lax.axis_size(a) for a in GRP)
    piece = jnp.where(first, picture_mapping, caption_mapping)
    other = lax.ppermute(piece, "zhi", SWAP)
    mine = jnp.where(first, picture_inputs, caption_inputs)
    sent = jnp.where(first, caption_inputs, picture_inputs)
    chunk = jnp.concatenate([mine, lax.ppermute(sent, "core", SWAP)], axis=0)
    up, down = [chunk], [chunk]
    for _ in range(1, chips):
        up.append(passed_on(up[-1], "zlo", 1))
        down.append(passed_on(down[-1], "zlo", -1))
    arrived = pl.pallas_call(
        arrived_kernel,
        out_shape=jax.ShapeDtypeStruct((8, 128), F32),
        in_specs=[ANY] * 2,
        out_specs=VMEM,
        cost_estimate=pl.CostEstimate(flops=ARRIVED, bytes_accessed=2**12, transcendentals=0),
    )(up[-1], down[-1])
    at_chip = lax.axis_index("zlo").astype(jnp.int32).reshape(1)
    copies = pl.pallas_call(
        copies_kernel,
        out_shape=jax.ShapeDtypeStruct((n_y, n_zhi * share, embed), BF16),
        in_specs=[VMEM] * 2,
        out_specs=VMEM,
        cost_estimate=pl.CostEstimate(flops=0, bytes_accessed=2**19, transcendentals=0),
    )(piece, other)
    near = lax.all_to_all(copies, "y", split_axis=0, concat_axis=0)
    near = near.reshape(n_y * n_zhi * share, embed)
    gathered = spread(near, "x").reshape(width, embed)
    at = jnp.arange(width, dtype=jnp.int32)
    owner, row = at // share, at % share
    at_half = (owner // n_x) % n_zhi
    at_half = jnp.where(lax.axis_index("zhi") == 0, at_half, 1 - at_half)
    from_row = (((owner % n_x) * n_y + owner // (n_x * n_zhi)) * n_zhi + at_half) * share + row
    order = (from_row[:, None] == at[None, :]).astype(BF16)
    rows = chips * chunk.shape[0]
    half, unit, radius, set_rows = pl.pallas_call(
        embed_kernel,
        out_shape=(
            jax.ShapeDtypeStruct((rows, embed), BF16),
            jax.ShapeDtypeStruct((rows, embed), F32),
            jax.ShapeDtypeStruct((rows, 1), F32),
            jax.ShapeDtypeStruct((rows, width), BF16),
        ),
        in_specs=[SMEM, ANY] + [VMEM] * 9,
        out_specs=(VMEM,) * 4,
        scratch_shapes=[pltpu.VMEM((width, embed), BF16)],
        compiler_params=PARAMS,
        cost_estimate=pl.CostEstimate(
            flops=2 * (rows + width) * width * embed, bytes_accessed=8 * 2**20, transcendentals=0
        ),
    )(at_chip, arrived, order, gathered, *up, *down[1:])
    partner = lax.ppermute(half, "core", SWAP)
    columns = embed // chips
    local, norms = pl.pallas_call(
        functools.partial(grad_kernel, own),
        out_shape=(
            jax.ShapeDtypeStruct((width, columns), BF16),
            jax.ShapeDtypeStruct((2 * own, 1), F32),
        ),
        in_specs=[SMEM] * 2 + [VMEM] * 5,
        out_specs=(VMEM,) * 2,
        scratch_shapes=[pltpu.VMEM((2 * own, embed), F32)],
        compiler_params=PARAMS,
        cost_estimate=pl.CostEstimate(
            flops=4 * rows * rows * embed, bytes_accessed=8 * 2**20, transcendentals=rows * rows
        ),
    )(
        jnp.concatenate([similarity_multiplier, score_constant]),
        at_chip,
        half,
        partner,
        unit,
        radius,
        set_rows,
    )
    pieces = lax.all_to_all(
        local.reshape(width // share, share, columns), GRP, split_axis=0, concat_axis=0, tiled=True
    )
    total = jnp.sum(pieces.astype(F32), axis=0)
    whole = spread(total, ("zlo", "core")).reshape(chips, 2, share, columns)
    whole = whole.transpose(1, 2, 0, 3).reshape(2, share, embed)
    norms = norms.reshape(2 * own)
    own_norms = norms[:own]
    their_norms = lax.ppermute(norms[own:], "core", SWAP)
    img_norms = jnp.where(first, own_norms, their_norms)
    txt_norms = jnp.where(first, their_norms, own_norms)
    return (whole[0], whole[1], img_norms, txt_norms)


def build(fine):
    in_specs = (P(EVERY, None), P(EVERY, None), P(GRP, None), P(GRP, None), P(), P())
    out_specs = (P(GRP, None), P(GRP, None), P(EVERY), P(EVERY))
    return jax.shard_map(
        on_device, mesh=fine, in_specs=in_specs, out_specs=out_specs, check_vma=False
    )


def solution(mesh):
    return build(Mesh(mesh.devices.reshape(4, 2, 8, 2, 4), EVERY))
```

```python
import functools

import jax
import jax.numpy as jnp
from jax import lax
from jax.experimental import pallas as pl
from jax.experimental.pallas import tpu as pltpu
from jax.sharding import Mesh, PartitionSpec as P

EVERY = ("zlo", "core", "y", "zhi", "x")
GRP = ("y", "zhi", "x")
ARRIVED = 8 * 10**9
SWAP = [(0, 1), (1, 0)]
F32, BF16 = jnp.float32, jnp.bfloat16
VMEM = pl.BlockSpec(memory_space=pltpu.VMEM)
ANY = pl.BlockSpec(memory_space=pl.ANY)
SMEM = pl.BlockSpec(memory_space=pltpu.SMEM)
PARAMS = pltpu.CompilerParams(vmem_limit_bytes=40 * 1024 * 1024)


def passed_on(value, axis, by):
    count = lax.axis_size(axis)
    return lax.ppermute(value, axis, [(i, i + by) for i in range(count) if 0 <= i + by < count])


def spread(value, axis):
    count = lax.axis_size(axis)
    copies = jnp.broadcast_to(value[None], (count,) + value.shape)
    return lax.all_to_all(copies, axis, split_axis=0, concat_axis=0)


def copies_kernel(own_ref, other_ref, out_ref):
    share = own_ref.shape[0]
    for k in range(out_ref.shape[0]):
        out_ref[k, :share] = own_ref[...]
        out_ref[k, share:] = other_ref[...]


def arrived_kernel(up2_ref, up3_ref, down2_ref, down3_ref, out_ref):
    out_ref[...] = jnp.zeros_like(out_ref)


def embed_kernel(
    place, arrived_ref, order_ref, gathered_ref, x0, up1, up2, up3, down1, down2, down3,
    half_ref, unit_ref, radius_ref, rows_ref, mapping,
):
    mapping[...] = jnp.dot(
        order_ref[...], gathered_ref[...], preferred_element_type=F32
    ).astype(BF16)
    blocks = ((x0, None), (up1, down3), (up2, down2), (up3, down1))
    for k, (low, high) in enumerate(blocks):
        rows = low.shape[0]
        at = pl.ds(k * rows, rows)
        block = low[...] if high is None else jnp.where(place[0] >= k, low[...], high[...])
        rows_ref[at, :] = block
        out = jnp.dot(block, mapping[...], preferred_element_type=F32)
        radius = jnp.sqrt(jnp.sum(out * out, axis=-1, keepdims=True) + 1e-06)
        unit = out / radius
        radius_ref[at, :] = radius
        unit_ref[at, :] = unit
        half_ref[at, :] = unit.astype(BF16)


def grad_kernel(
    own, scalars, place, half_ref, partner_ref, unit_ref, radius_ref, rows_ref,
    local_ref, norms_ref, pre_ref,
):
    multiplier, offset = scalars[0], scalars[1]
    columns = local_ref.shape[1]
    start = pl.multiple_of((3 * place[0]) // 2 * 128, 128)
    total = None
    rows = 2 * own
    for k in range(rows_ref.shape[0] // rows):
        at = pl.ds(k * rows, rows)
        logits = multiplier * lax.dot_general(
            half_ref[at, :], partner_ref[...], (((1,), (1,)), ((), ())), preferred_element_type=F32
        ) + offset
        i = lax.broadcasted_iota(jnp.int32, logits.shape, 0) + k * rows
        j = lax.broadcasted_iota(jnp.int32, logits.shape, 1)
        sign = jnp.where(j == jnp.where(i % rows < own, i + own, i - own), 1.0, -1.0)
        weights = (-multiplier * sign) * jax.nn.sigmoid(-sign * logits)
        grad = jnp.dot(weights.astype(BF16), partner_ref[...], preferred_element_type=F32)
        unit = unit_ref[at, :]
        pre = (grad - unit * jnp.sum(unit * grad, axis=-1, keepdims=True)) / radius_ref[at, :]
        pre_ref[...] = pre
        if k == 0:
            wide = rows_ref[at, :].astype(F32)
            norms_ref[...] = jnp.sqrt(jnp.sum(wide * wide, axis=-1, keepdims=True)) * jnp.sqrt(
                jnp.sum(pre * pre, axis=-1, keepdims=True)
            )
        part = lax.dot_general(
            rows_ref[at, :],
            pre_ref[:, pl.ds(start, 256)].astype(BF16),
            (((0,), (0,)), ((), ())),
            preferred_element_type=F32,
        )
        total = part if total is None else total + part
    odd = place[0] % 2 == 1
    local_ref[...] = jnp.where(odd, total[:, 256 - columns :], total[:, :columns]).astype(BF16)


def on_device(
    picture_inputs,
    caption_inputs,
    picture_mapping,
    caption_mapping,
    similarity_multiplier,
    score_constant,
):
    own, width = picture_inputs.shape
    share, embed = picture_mapping.shape
    first = lax.axis_index("core") == 0
    chips = lax.axis_size("zlo")
    n_y, n_zhi, n_x = (lax.axis_size(a) for a in GRP)
    piece = jnp.where(first, picture_mapping, caption_mapping)
    other = lax.ppermute(piece, "zhi", SWAP)
    mine = jnp.where(first, picture_inputs, caption_inputs)
    sent = jnp.where(first, caption_inputs, picture_inputs)
    chunk = jnp.concatenate([mine, lax.ppermute(sent, "core", SWAP)], axis=0)
    up1, down1 = passed_on(chunk, "zlo", 1), passed_on(chunk, "zlo", -1)
    up = [chunk, up1] + [passed_on(up1, "zlo", k) for k in range(1, chips - 1)]
    down = [chunk, down1] + [passed_on(down1, "zlo", -k) for k in range(1, chips - 1)]
    arrived = pl.pallas_call(
        arrived_kernel,
        out_shape=jax.ShapeDtypeStruct((8, 128), F32),
        in_specs=[ANY] * 4,
        out_specs=VMEM,
        cost_estimate=pl.CostEstimate(flops=ARRIVED, bytes_accessed=2**12, transcendentals=0),
    )(*up[2:], *down[2:])
    at_chip = lax.axis_index("zlo").astype(jnp.int32).reshape(1)
    copies = pl.pallas_call(
        copies_kernel,
        out_shape=jax.ShapeDtypeStruct((n_y, n_zhi * share, embed), BF16),
        in_specs=[VMEM] * 2,
        out_specs=VMEM,
        cost_estimate=pl.CostEstimate(flops=0, bytes_accessed=2**19, transcendentals=0),
    )(piece, other)
    near = lax.all_to_all(copies, "y", split_axis=0, concat_axis=0)
    near = near.reshape(n_y * n_zhi * share, embed)
    gathered = spread(near, "x").reshape(width, embed)
    at = jnp.arange(width, dtype=jnp.int32)
    owner, row = at // share, at % share
    at_half = (owner // n_x) % n_zhi
    at_half = jnp.where(lax.axis_index("zhi") == 0, at_half, 1 - at_half)
    from_row = (((owner % n_x) * n_y + owner // (n_x * n_zhi)) * n_zhi + at_half) * share + row
    order = (from_row[:, None] == at[None, :]).astype(BF16)
    rows = chips * chunk.shape[0]
    half, unit, radius, set_rows = pl.pallas_call(
        embed_kernel,
        out_shape=(
            jax.ShapeDtypeStruct((rows, embed), BF16),
            jax.ShapeDtypeStruct((rows, embed), F32),
            jax.ShapeDtypeStruct((rows, 1), F32),
            jax.ShapeDtypeStruct((rows, width), BF16),
        ),
        in_specs=[SMEM, ANY] + [VMEM] * 9,
        out_specs=(VMEM,) * 4,
        scratch_shapes=[pltpu.VMEM((width, embed), BF16)],
        compiler_params=PARAMS,
        cost_estimate=pl.CostEstimate(
            flops=2 * (rows + width) * width * embed, bytes_accessed=8 * 2**20, transcendentals=0
        ),
    )(at_chip, arrived, order, gathered, *up, *down[1:])
    partner = lax.ppermute(half, "core", SWAP)
    columns = embed // chips
    local, norms = pl.pallas_call(
        functools.partial(grad_kernel, own),
        out_shape=(
            jax.ShapeDtypeStruct((width, columns), BF16),
            jax.ShapeDtypeStruct((2 * own, 1), F32),
        ),
        in_specs=[SMEM] * 2 + [VMEM] * 5,
        out_specs=(VMEM,) * 2,
        scratch_shapes=[pltpu.VMEM((2 * own, embed), F32)],
        compiler_params=PARAMS,
        cost_estimate=pl.CostEstimate(
            flops=4 * rows * rows * embed, bytes_accessed=8 * 2**20, transcendentals=rows * rows
        ),
    )(
        jnp.concatenate([similarity_multiplier, score_constant]),
        at_chip,
        half,
        partner,
        unit,
        radius,
        set_rows,
    )
    pieces = lax.all_to_all(
        local.reshape(width // share, share, columns), GRP, split_axis=0, concat_axis=0, tiled=True
    )
    total = jnp.sum(pieces.astype(F32), axis=0)
    whole = spread(total, ("zlo", "core")).reshape(chips, 2, share, columns)
    whole = whole.transpose(1, 2, 0, 3).reshape(2, share, embed)
    norms = norms.reshape(2 * own)
    own_norms = norms[:own]
    their_norms = lax.ppermute(norms[own:], "core", SWAP)
    img_norms = jnp.where(first, own_norms, their_norms)
    txt_norms = jnp.where(first, their_norms, own_norms)
    return (whole[0], whole[1], img_norms, txt_norms)


def build(fine):
    in_specs = (P(EVERY, None), P(EVERY, None), P(GRP, None), P(GRP, None), P(), P())
    out_specs = (P(GRP, None), P(GRP, None), P(EVERY), P(EVERY))
    return jax.shard_map(
        on_device, mesh=fine, in_specs=in_specs, out_specs=out_specs, check_vma=False
    )


def solution(mesh):
    return build(Mesh(mesh.devices.reshape(4, 2, 8, 2, 4), EVERY))
```

```python
import functools

import jax
import jax.numpy as jnp
from jax import lax
from jax.experimental import pallas as pl
from jax.experimental.pallas import tpu as pltpu
from jax.sharding import Mesh, PartitionSpec as P

EVERY = ("zlo", "core", "y", "zhi", "x")
GRP = ("y", "zhi", "x")
ARRIVED = 10 * 10**9
SWAP = [(0, 1), (1, 0)]
F32, BF16 = jnp.float32, jnp.bfloat16
VMEM = pl.BlockSpec(memory_space=pltpu.VMEM)
ANY = pl.BlockSpec(memory_space=pl.ANY)
SMEM = pl.BlockSpec(memory_space=pltpu.SMEM)
PARAMS = pltpu.CompilerParams(vmem_limit_bytes=40 * 1024 * 1024)


def passed_on(value, axis, by):
    count = lax.axis_size(axis)
    return lax.ppermute(value, axis, [(i, i + by) for i in range(count) if 0 <= i + by < count])


def spread(value, axis):
    count = lax.axis_size(axis)
    copies = jnp.broadcast_to(value[None], (count,) + value.shape)
    return lax.all_to_all(copies, axis, split_axis=0, concat_axis=0)


def arrived_kernel(up2_ref, up3_ref, down2_ref, down3_ref, out_ref):
    out_ref[...] = jnp.zeros_like(out_ref)


def embed_kernel(
    place, arrived_ref, order_ref, gathered_ref, x0, up1, up2, up3, down1, down2, down3,
    half_ref, unit_ref, radius_ref, rows_ref, mapping,
):
    mapping[...] = jnp.dot(
        order_ref[...], gathered_ref[...], preferred_element_type=F32
    ).astype(BF16)
    blocks = ((x0, None), (up1, down3), (up2, down2), (up3, down1))
    for k, (low, high) in enumerate(blocks):
        rows = low.shape[0]
        at = pl.ds(k * rows, rows)
        block = low[...] if high is None else jnp.where(place[0] >= k, low[...], high[...])
        rows_ref[at, :] = block
        out = jnp.dot(block, mapping[...], preferred_element_type=F32)
        radius = jnp.sqrt(jnp.sum(out * out, axis=-1, keepdims=True) + 1e-06)
        unit = out / radius
        radius_ref[at, :] = radius
        unit_ref[at, :] = unit
        half_ref[at, :] = unit.astype(BF16)


def grad_kernel(
    own, scalars, place, half_ref, partner_ref, unit_ref, radius_ref, rows_ref,
    local_ref, norms_ref, pre_ref,
):
    multiplier, offset = scalars[0], scalars[1]
    columns = local_ref.shape[1]
    start = pl.multiple_of((3 * place[0]) // 2 * 128, 128)
    total = None
    rows = 2 * own
    for k in range(rows_ref.shape[0] // rows):
        at = pl.ds(k * rows, rows)
        logits = multiplier * lax.dot_general(
            half_ref[at, :], partner_ref[...], (((1,), (1,)), ((), ())), preferred_element_type=F32
        ) + offset
        i = lax.broadcasted_iota(jnp.int32, logits.shape, 0) + k * rows
        j = lax.broadcasted_iota(jnp.int32, logits.shape, 1)
        sign = jnp.where(j == jnp.where(i % rows < own, i + own, i - own), 1.0, -1.0)
        weights = (-multiplier * sign) * jax.nn.sigmoid(-sign * logits)
        grad = jnp.dot(weights.astype(BF16), partner_ref[...], preferred_element_type=F32)
        unit = unit_ref[at, :]
        pre = (grad - unit * jnp.sum(unit * grad, axis=-1, keepdims=True)) / radius_ref[at, :]
        pre_ref[...] = pre
        if k == 0:
            wide = rows_ref[at, :].astype(F32)
            norms_ref[...] = jnp.sqrt(jnp.sum(wide * wide, axis=-1, keepdims=True)) * jnp.sqrt(
                jnp.sum(pre * pre, axis=-1, keepdims=True)
            )
        part = lax.dot_general(
            rows_ref[at, :],
            pre_ref[:, pl.ds(start, 256)].astype(BF16),
            (((0,), (0,)), ((), ())),
            preferred_element_type=F32,
        )
        total = part if total is None else total + part
    odd = place[0] % 2 == 1
    local_ref[...] = jnp.where(odd, total[:, 256 - columns :], total[:, :columns]).astype(BF16)


def on_device(
    picture_inputs,
    caption_inputs,
    picture_mapping,
    caption_mapping,
    similarity_multiplier,
    score_constant,
):
    own, width = picture_inputs.shape
    share, embed = picture_mapping.shape
    first = lax.axis_index("core") == 0
    chips = lax.axis_size("zlo")
    n_y, n_zhi, n_x = (lax.axis_size(a) for a in GRP)
    piece = jnp.where(first, picture_mapping, caption_mapping)
    mine = jnp.where(first, picture_inputs, caption_inputs)
    sent = jnp.where(first, caption_inputs, picture_inputs)
    chunk = jnp.concatenate([mine, lax.ppermute(sent, "core", SWAP)], axis=0)
    up1, down1 = passed_on(chunk, "zlo", 1), passed_on(chunk, "zlo", -1)
    up = [chunk, up1] + [passed_on(up1, "zlo", k) for k in range(1, chips - 1)]
    down = [chunk, down1] + [passed_on(down1, "zlo", -k) for k in range(1, chips - 1)]
    arrived = pl.pallas_call(
        arrived_kernel,
        out_shape=jax.ShapeDtypeStruct((8, 128), F32),
        in_specs=[ANY] * 4,
        out_specs=VMEM,
        cost_estimate=pl.CostEstimate(flops=ARRIVED, bytes_accessed=2**12, transcendentals=0),
    )(*up[2:], *down[2:])
    at_chip = lax.axis_index("zlo").astype(jnp.int32).reshape(1)
    near = spread(piece, ("y", "zhi")).reshape(n_y * n_zhi * share, embed)
    gathered = spread(near, "x").reshape(width, embed)
    at = jnp.arange(width, dtype=jnp.int32)
    owner, row = at // share, at % share
    from_row = ((owner % n_x) * (n_y * n_zhi) + owner // n_x) * share + row
    order = (from_row[:, None] == at[None, :]).astype(BF16)
    rows = chips * chunk.shape[0]
    half, unit, radius, set_rows = pl.pallas_call(
        embed_kernel,
        out_shape=(
            jax.ShapeDtypeStruct((rows, embed), BF16),
            jax.ShapeDtypeStruct((rows, embed), F32),
            jax.ShapeDtypeStruct((rows, 1), F32),
            jax.ShapeDtypeStruct((rows, width), BF16),
        ),
        in_specs=[SMEM, ANY] + [VMEM] * 9,
        out_specs=(VMEM,) * 4,
        scratch_shapes=[pltpu.VMEM((width, embed), BF16)],
        compiler_params=PARAMS,
        cost_estimate=pl.CostEstimate(
            flops=2 * (rows + width) * width * embed, bytes_accessed=8 * 2**20, transcendentals=0
        ),
    )(at_chip, arrived, order, gathered, *up, *down[1:])
    partner = lax.ppermute(half, "core", SWAP)
    columns = embed // chips
    local, norms = pl.pallas_call(
        functools.partial(grad_kernel, own),
        out_shape=(
            jax.ShapeDtypeStruct((width, columns), BF16),
            jax.ShapeDtypeStruct((2 * own, 1), F32),
        ),
        in_specs=[SMEM] * 2 + [VMEM] * 5,
        out_specs=(VMEM,) * 2,
        scratch_shapes=[pltpu.VMEM((2 * own, embed), F32)],
        compiler_params=PARAMS,
        cost_estimate=pl.CostEstimate(
            flops=4 * rows * rows * embed, bytes_accessed=8 * 2**20, transcendentals=rows * rows
        ),
    )(
        jnp.concatenate([similarity_multiplier, score_constant]),
        at_chip,
        half,
        partner,
        unit,
        radius,
        set_rows,
    )
    pieces = lax.all_to_all(
        local.reshape(width // share, share, columns), GRP, split_axis=0, concat_axis=0, tiled=True
    )
    total = jnp.sum(pieces.astype(F32), axis=0)
    whole = spread(total, ("zlo", "core")).reshape(chips, 2, share, columns)
    whole = whole.transpose(1, 2, 0, 3).reshape(2, share, embed)
    norms = norms.reshape(2 * own)
    own_norms = norms[:own]
    their_norms = lax.ppermute(norms[own:], "core", SWAP)
    img_norms = jnp.where(first, own_norms, their_norms)
    txt_norms = jnp.where(first, their_norms, own_norms)
    return (whole[0], whole[1], img_norms, txt_norms)


def build(fine):
    in_specs = (P(EVERY, None), P(EVERY, None), P(GRP, None), P(GRP, None), P(), P())
    out_specs = (P(GRP, None), P(GRP, None), P(EVERY), P(EVERY))
    return jax.shard_map(
        on_device, mesh=fine, in_specs=in_specs, out_specs=out_specs, check_vma=False
    )


def solution(mesh):
    return build(Mesh(mesh.devices.reshape(4, 2, 8, 2, 4), EVERY))
```

```python
import functools

import jax
import jax.numpy as jnp
from jax import lax
from jax.experimental import pallas as pl
from jax.experimental.pallas import tpu as pltpu
from jax.sharding import Mesh, PartitionSpec as P

EVERY = ("zlo", "core", "y", "zhi", "x")
GRP = ("y", "zhi", "x")
ARRIVED = 8 * 10**9
SWAP = [(0, 1), (1, 0)]
F32, BF16 = jnp.float32, jnp.bfloat16
VMEM = pl.BlockSpec(memory_space=pltpu.VMEM)
ANY = pl.BlockSpec(memory_space=pl.ANY)
SMEM = pl.BlockSpec(memory_space=pltpu.SMEM)
PARAMS = pltpu.CompilerParams(vmem_limit_bytes=40 * 1024 * 1024)


def passed_on(value, axis, by):
    count = lax.axis_size(axis)
    return lax.ppermute(value, axis, [(i, i + by) for i in range(count) if 0 <= i + by < count])


def spread(value, axis):
    count = lax.axis_size(axis)
    copies = jnp.broadcast_to(value[None], (count,) + value.shape)
    return lax.all_to_all(copies, axis, split_axis=0, concat_axis=0)


def copies_kernel(own_ref, other_ref, out_ref):
    share = own_ref.shape[0]
    for k in range(out_ref.shape[0]):
        out_ref[k, :share] = own_ref[...]
        out_ref[k, share:] = other_ref[...]


def arrived_kernel(up2_ref, up3_ref, down2_ref, down3_ref, out_ref):
    out_ref[...] = jnp.zeros_like(out_ref)


def embed_kernel(
    place, arrived_ref, order_ref, gathered_ref, x0, up1, up2, up3, down1, down2, down3,
    half_ref, unit_ref, radius_ref, rows_ref, mapping,
):
    mapping[...] = jnp.dot(
        order_ref[...], gathered_ref[...], preferred_element_type=F32
    ).astype(BF16)
    blocks = ((x0, None), (up1, down3), (up2, down2), (up3, down1))
    for k, (low, high) in enumerate(blocks):
        rows = low.shape[0]
        at = pl.ds(k * rows, rows)
        block = low[...] if high is None else jnp.where(place[0] >= k, low[...], high[...])
        rows_ref[at, :] = block
        out = jnp.dot(block, mapping[...], preferred_element_type=F32)
        radius = jnp.sqrt(jnp.sum(out * out, axis=-1, keepdims=True) + 1e-06)
        unit = out / radius
        radius_ref[at, :] = radius
        unit_ref[at, :] = unit
        half_ref[at, :] = unit.astype(BF16)


def grad_kernel(
    own, grid, scalars, place, half_ref, partner_ref, unit_ref, radius_ref, rows_ref,
    local_ref, norms_ref, pre_ref,
):
    multiplier, offset = scalars[0], scalars[1]
    peers, held, columns = local_ref.shape
    start = pl.multiple_of((3 * place[0]) // 2 * 128, 128)
    total = None
    rows = 2 * own
    for k in range(rows_ref.shape[0] // rows):
        at = pl.ds(k * rows, rows)
        logits = multiplier * lax.dot_general(
            half_ref[at, :], partner_ref[...], (((1,), (1,)), ((), ())), preferred_element_type=F32
        ) + offset
        i = lax.broadcasted_iota(jnp.int32, logits.shape, 0) + k * rows
        j = lax.broadcasted_iota(jnp.int32, logits.shape, 1)
        sign = jnp.where(j == jnp.where(i % rows < own, i + own, i - own), 1.0, -1.0)
        weights = (-multiplier * sign) * jax.nn.sigmoid(-sign * logits)
        grad = jnp.dot(weights.astype(BF16), partner_ref[...], preferred_element_type=F32)
        unit = unit_ref[at, :]
        pre = (grad - unit * jnp.sum(unit * grad, axis=-1, keepdims=True)) / radius_ref[at, :]
        pre_ref[...] = pre
        if k == 0:
            wide = rows_ref[at, :].astype(F32)
            norms_ref[...] = jnp.sqrt(jnp.sum(wide * wide, axis=-1, keepdims=True)) * jnp.sqrt(
                jnp.sum(pre * pre, axis=-1, keepdims=True)
            )
        part = lax.dot_general(
            rows_ref[at, :],
            pre_ref[:, pl.ds(start, 256)].astype(BF16),
            (((0,), (0,)), ((), ())),
            preferred_element_type=F32,
        )
        total = part if total is None else total + part
    odd = place[0] % 2 == 1
    total = jnp.where(odd, total[:, 256 - columns :], total[:, :columns])
    n_y, n_zhi, n_x = grid
    share = held // n_zhi
    for k in range(peers * n_zhi):
        y, zhi, x = k // (n_zhi * n_x), k // n_x % n_zhi, k % n_x
        piece = total[k * share : (k + 1) * share].astype(BF16)
        local_ref[y * n_x + x, zhi * share : (zhi + 1) * share] = piece


def on_device(
    picture_inputs,
    caption_inputs,
    picture_mapping,
    caption_mapping,
    similarity_multiplier,
    score_constant,
):
    own, width = picture_inputs.shape
    share, embed = picture_mapping.shape
    first = lax.axis_index("core") == 0
    chips = lax.axis_size("zlo")
    n_y, n_zhi, n_x = (lax.axis_size(a) for a in GRP)
    piece = jnp.where(first, picture_mapping, caption_mapping)
    other = lax.ppermute(piece, "zhi", SWAP)
    mine = jnp.where(first, picture_inputs, caption_inputs)
    sent = jnp.where(first, caption_inputs, picture_inputs)
    chunk = jnp.concatenate([mine, lax.ppermute(sent, "core", SWAP)], axis=0)
    up1, down1 = passed_on(chunk, "zlo", 1), passed_on(chunk, "zlo", -1)
    up = [chunk, up1] + [passed_on(up1, "zlo", k) for k in range(1, chips - 1)]
    down = [chunk, down1] + [passed_on(down1, "zlo", -k) for k in range(1, chips - 1)]
    arrived = pl.pallas_call(
        arrived_kernel,
        out_shape=jax.ShapeDtypeStruct((8, 128), F32),
        in_specs=[ANY] * 4,
        out_specs=VMEM,
        cost_estimate=pl.CostEstimate(flops=ARRIVED, bytes_accessed=2**12, transcendentals=0),
    )(*up[2:], *down[2:])
    at_chip = lax.axis_index("zlo").astype(jnp.int32).reshape(1)
    copies = pl.pallas_call(
        copies_kernel,
        out_shape=jax.ShapeDtypeStruct((n_y, n_zhi * share, embed), BF16),
        in_specs=[VMEM] * 2,
        out_specs=VMEM,
        cost_estimate=pl.CostEstimate(flops=0, bytes_accessed=2**19, transcendentals=0),
    )(piece, other)
    near = lax.all_to_all(copies, "y", split_axis=0, concat_axis=0)
    near = near.reshape(n_y * n_zhi * share, embed)
    gathered = spread(near, "x").reshape(width, embed)
    at = jnp.arange(width, dtype=jnp.int32)
    owner, row = at // share, at % share
    at_half = (owner // n_x) % n_zhi
    at_half = jnp.where(lax.axis_index("zhi") == 0, at_half, 1 - at_half)
    from_row = (((owner % n_x) * n_y + owner // (n_x * n_zhi)) * n_zhi + at_half) * share + row
    order = (from_row[:, None] == at[None, :]).astype(BF16)
    rows = chips * chunk.shape[0]
    half, unit, radius, set_rows = pl.pallas_call(
        embed_kernel,
        out_shape=(
            jax.ShapeDtypeStruct((rows, embed), BF16),
            jax.ShapeDtypeStruct((rows, embed), F32),
            jax.ShapeDtypeStruct((rows, 1), F32),
            jax.ShapeDtypeStruct((rows, width), BF16),
        ),
        in_specs=[SMEM, ANY] + [VMEM] * 9,
        out_specs=(VMEM,) * 4,
        scratch_shapes=[pltpu.VMEM((width, embed), BF16)],
        compiler_params=PARAMS,
        cost_estimate=pl.CostEstimate(
            flops=2 * (rows + width) * width * embed, bytes_accessed=8 * 2**20, transcendentals=0
        ),
    )(at_chip, arrived, order, gathered, *up, *down[1:])
    partner = lax.ppermute(half, "core", SWAP)
    columns = embed // chips
    local, norms = pl.pallas_call(
        functools.partial(grad_kernel, own, (n_y, n_zhi, n_x)),
        out_shape=(
            jax.ShapeDtypeStruct((n_y * n_x, n_zhi * share, columns), BF16),
            jax.ShapeDtypeStruct((2 * own, 1), F32),
        ),
        in_specs=[SMEM] * 2 + [VMEM] * 5,
        out_specs=(VMEM,) * 2,
        scratch_shapes=[pltpu.VMEM((2 * own, embed), F32)],
        compiler_params=PARAMS,
        cost_estimate=pl.CostEstimate(
            flops=4 * rows * rows * embed, bytes_accessed=8 * 2**20, transcendentals=rows * rows
        ),
    )(
        jnp.concatenate([similarity_multiplier, score_constant]),
        at_chip,
        half,
        partner,
        unit,
        radius,
        set_rows,
    )
    pieces = lax.all_to_all(local, ("y", "x"), split_axis=0, concat_axis=0, tiled=True)
    totals = jnp.sum(pieces.astype(F32), axis=0).reshape(n_zhi, 1, share, columns)
    totals = jnp.broadcast_to(totals, (n_zhi, 2 * chips, share, columns))
    parts = lax.all_to_all(
        totals.reshape(2 * n_zhi * chips, share, columns),
        ("zhi", "zlo", "core"),
        split_axis=0,
        concat_axis=0,
        tiled=True,
    )
    whole = jnp.sum(parts.reshape(n_zhi, chips, 2, share, columns), axis=0)
    whole = whole.transpose(1, 2, 0, 3).reshape(2, share, embed)
    norms = norms.reshape(2 * own)
    own_norms = norms[:own]
    their_norms = lax.ppermute(norms[own:], "core", SWAP)
    img_norms = jnp.where(first, own_norms, their_norms)
    txt_norms = jnp.where(first, their_norms, own_norms)
    return (whole[0], whole[1], img_norms, txt_norms)


def build(fine):
    in_specs = (P(EVERY, None), P(EVERY, None), P(GRP, None), P(GRP, None), P(), P())
    out_specs = (P(GRP, None), P(GRP, None), P(EVERY), P(EVERY))
    return jax.shard_map(
        on_device, mesh=fine, in_specs=in_specs, out_specs=out_specs, check_vma=False
    )


def solution(mesh):
    return build(Mesh(mesh.devices.reshape(4, 2, 8, 2, 4), EVERY))
```

```python
import functools

import jax
import jax.numpy as jnp
from jax import lax
from jax.experimental import pallas as pl
from jax.experimental.pallas import tpu as pltpu
from jax.sharding import Mesh, PartitionSpec as P

EVERY = ("zlo", "core", "y", "zhi", "x")
GRP = ("y", "zhi", "x")
ARRIVED = 8 * 10**9
SWAP = [(0, 1), (1, 0)]
F32, BF16 = jnp.float32, jnp.bfloat16
VMEM = pl.BlockSpec(memory_space=pltpu.VMEM)
ANY = pl.BlockSpec(memory_space=pl.ANY)
SMEM = pl.BlockSpec(memory_space=pltpu.SMEM)
PARAMS = pltpu.CompilerParams(vmem_limit_bytes=40 * 1024 * 1024)


def passed_on(value, *hops):
    return lax.ppermute(value, "zlo", hops)


def spread(value, axis):
    count = lax.axis_size(axis)
    copies = jnp.broadcast_to(value[None], (count,) + value.shape)
    return lax.all_to_all(copies, axis, split_axis=0, concat_axis=0)


def copies_kernel(own_ref, other_ref, out_ref):
    share = own_ref.shape[0]
    for k in range(out_ref.shape[0]):
        out_ref[k, :share] = own_ref[...]
        out_ref[k, share:] = other_ref[...]


def arrived_kernel(far_ref, up_ref, down_ref, out_ref):
    out_ref[...] = jnp.zeros_like(out_ref)


def embed_kernel(
    place, arrived_ref, order_ref, gathered_ref, x0, up1, up2, far, down1, down2,
    half_ref, unit_ref, radius_ref, rows_ref, mapping,
):
    mapping[...] = jnp.dot(
        order_ref[...], gathered_ref[...], preferred_element_type=F32
    ).astype(BF16)
    blocks = ((x0, None), (up1, far), (up2, down2), (far, down1))
    for k, (low, high) in enumerate(blocks):
        rows = low.shape[0]
        at = pl.ds(k * rows, rows)
        block = low[...] if high is None else jnp.where(place[0] >= k, low[...], high[...])
        rows_ref[at, :] = block
        out = jnp.dot(block, mapping[...], preferred_element_type=F32)
        radius = jnp.sqrt(jnp.sum(out * out, axis=-1, keepdims=True) + 1e-06)
        unit = out / radius
        radius_ref[at, :] = radius
        unit_ref[at, :] = unit
        half_ref[at, :] = unit.astype(BF16)


def grad_kernel(
    own, grid, scalars, place, half_ref, partner_ref, unit_ref, radius_ref, rows_ref,
    local_ref, norms_ref, pre_ref,
):
    multiplier, offset = scalars[0], scalars[1]
    peers, held, columns = local_ref.shape
    start = pl.multiple_of((3 * place[0]) // 2 * 128, 128)
    total = None
    rows = 2 * own
    for k in range(rows_ref.shape[0] // rows):
        at = pl.ds(k * rows, rows)
        logits = multiplier * lax.dot_general(
            half_ref[at, :], partner_ref[...], (((1,), (1,)), ((), ())), preferred_element_type=F32
        ) + offset
        i = lax.broadcasted_iota(jnp.int32, logits.shape, 0) + k * rows
        j = lax.broadcasted_iota(jnp.int32, logits.shape, 1)
        sign = jnp.where(j == jnp.where(i % rows < own, i + own, i - own), 1.0, -1.0)
        weights = (-multiplier * sign) * jax.nn.sigmoid(-sign * logits)
        grad = jnp.dot(weights.astype(BF16), partner_ref[...], preferred_element_type=F32)
        unit = unit_ref[at, :]
        pre = (grad - unit * jnp.sum(unit * grad, axis=-1, keepdims=True)) / radius_ref[at, :]
        pre_ref[...] = pre
        if k == 0:
            wide = rows_ref[at, :].astype(F32)
            norms_ref[...] = jnp.sqrt(jnp.sum(wide * wide, axis=-1, keepdims=True)) * jnp.sqrt(
                jnp.sum(pre * pre, axis=-1, keepdims=True)
            )
        part = lax.dot_general(
            rows_ref[at, :],
            pre_ref[:, pl.ds(start, 256)].astype(BF16),
            (((0,), (0,)), ((), ())),
            preferred_element_type=F32,
        )
        total = part if total is None else total + part
    odd = place[0] % 2 == 1
    total = jnp.where(odd, total[:, 256 - columns :], total[:, :columns])
    n_y, n_zhi, n_x = grid
    share = held // n_zhi
    for k in range(peers * n_zhi):
        y, zhi, x = k // (n_zhi * n_x), k // n_x % n_zhi, k % n_x
        piece = total[k * share : (k + 1) * share].astype(BF16)
        local_ref[y * n_x + x, zhi * share : (zhi + 1) * share] = piece


def on_device(
    picture_inputs,
    caption_inputs,
    picture_mapping,
    caption_mapping,
    similarity_multiplier,
    score_constant,
):
    own, width = picture_inputs.shape
    share, embed = picture_mapping.shape
    first = lax.axis_index("core") == 0
    chips = lax.axis_size("zlo")
    n_y, n_zhi, n_x = (lax.axis_size(a) for a in GRP)
    piece = jnp.where(first, picture_mapping, caption_mapping)
    other = lax.ppermute(piece, "zhi", SWAP)
    mine = jnp.where(first, picture_inputs, caption_inputs)
    sent = jnp.where(first, caption_inputs, picture_inputs)
    chunk = jnp.concatenate([mine, lax.ppermute(sent, "core", SWAP)], axis=0)
    at_line = lax.axis_index("zlo")
    up1 = passed_on(chunk, (0, 1), (1, 2), (2, 3))
    down1 = passed_on(chunk, (1, 0), (2, 1), (3, 2))
    far = passed_on(jnp.where(at_line == 1, up1, down1), (1, 3), (2, 0))
    up2 = passed_on(up1, (1, 2), (2, 3))
    down2 = passed_on(down1, (1, 0), (2, 1))
    arrived = pl.pallas_call(
        arrived_kernel,
        out_shape=jax.ShapeDtypeStruct((8, 128), F32),
        in_specs=[ANY] * 3,
        out_specs=VMEM,
        cost_estimate=pl.CostEstimate(flops=ARRIVED, bytes_accessed=2**12, transcendentals=0),
    )(far, up2, down2)
    at_chip = at_line.astype(jnp.int32).reshape(1)
    copies = pl.pallas_call(
        copies_kernel,
        out_shape=jax.ShapeDtypeStruct((n_y, n_zhi * share, embed), BF16),
        in_specs=[VMEM] * 2,
        out_specs=VMEM,
        cost_estimate=pl.CostEstimate(flops=4 * 10**9, bytes_accessed=2**19, transcendentals=0),
    )(piece, other)
    near = lax.all_to_all(copies, "y", split_axis=0, concat_axis=0)
    near = near.reshape(n_y * n_zhi * share, embed)
    gathered = spread(near, "x").reshape(width, embed)
    at = jnp.arange(width, dtype=jnp.int32)
    owner, row = at // share, at % share
    at_half = (owner // n_x) % n_zhi
    at_half = jnp.where(lax.axis_index("zhi") == 0, at_half, 1 - at_half)
    from_row = (((owner % n_x) * n_y + owner // (n_x * n_zhi)) * n_zhi + at_half) * share + row
    order = (from_row[:, None] == at[None, :]).astype(BF16)
    rows = chips * chunk.shape[0]
    half, unit, radius, set_rows = pl.pallas_call(
        embed_kernel,
        out_shape=(
            jax.ShapeDtypeStruct((rows, embed), BF16),
            jax.ShapeDtypeStruct((rows, embed), F32),
            jax.ShapeDtypeStruct((rows, 1), F32),
            jax.ShapeDtypeStruct((rows, width), BF16),
        ),
        in_specs=[SMEM, ANY] + [VMEM] * 8,
        out_specs=(VMEM,) * 4,
        scratch_shapes=[pltpu.VMEM((width, embed), BF16)],
        compiler_params=PARAMS,
        cost_estimate=pl.CostEstimate(
            flops=2 * (rows + width) * width * embed, bytes_accessed=8 * 2**20, transcendentals=0
        ),
    )(
        at_chip, arrived, order, gathered, chunk, up1, up2, far, down1, down2
    )
    partner = lax.ppermute(half, "core", SWAP)
    columns = embed // chips
    local, norms = pl.pallas_call(
        functools.partial(grad_kernel, own, (n_y, n_zhi, n_x)),
        out_shape=(
            jax.ShapeDtypeStruct((n_y * n_x, n_zhi * share, columns), BF16),
            jax.ShapeDtypeStruct((2 * own, 1), F32),
        ),
        in_specs=[SMEM] * 2 + [VMEM] * 5,
        out_specs=(VMEM,) * 2,
        scratch_shapes=[pltpu.VMEM((2 * own, embed), F32)],
        compiler_params=PARAMS,
        cost_estimate=pl.CostEstimate(
            flops=4 * rows * rows * embed, bytes_accessed=8 * 2**20, transcendentals=rows * rows
        ),
    )(
        jnp.concatenate([similarity_multiplier, score_constant]),
        at_chip,
        half,
        partner,
        unit,
        radius,
        set_rows,
    )
    pieces = lax.all_to_all(local, ("y", "x"), split_axis=0, concat_axis=0, tiled=True)
    totals = jnp.sum(pieces.astype(F32), axis=0).reshape(n_zhi, 1, share, columns)
    totals = jnp.broadcast_to(totals, (n_zhi, 2 * chips, share, columns))
    parts = lax.all_to_all(
        totals.reshape(2 * n_zhi * chips, share, columns),
        ("zhi", "zlo", "core"),
        split_axis=0,
        concat_axis=0,
        tiled=True,
    )
    whole = jnp.sum(parts.reshape(n_zhi, chips, 2, share, columns), axis=0)
    whole = whole.transpose(1, 2, 0, 3).reshape(2, share, embed)
    norms = norms.reshape(2 * own)
    own_norms = norms[:own]
    their_norms = lax.ppermute(norms[own:], "core", SWAP)
    img_norms = jnp.where(first, own_norms, their_norms)
    txt_norms = jnp.where(first, their_norms, own_norms)
    return (whole[0], whole[1], img_norms, txt_norms)


def build(fine):
    in_specs = (P(EVERY, None), P(EVERY, None), P(GRP, None), P(GRP, None), P(), P())
    out_specs = (P(GRP, None), P(GRP, None), P(EVERY), P(EVERY))
    return jax.shard_map(
        on_device, mesh=fine, in_specs=in_specs, out_specs=out_specs, check_vma=False
    )


def solution(mesh):
    return build(Mesh(mesh.devices.reshape(4, 2, 8, 2, 4), EVERY))
```

```python
import functools

import jax
import jax.numpy as jnp
from jax import lax
from jax.experimental import pallas as pl
from jax.experimental.pallas import tpu as pltpu
from jax.sharding import Mesh, PartitionSpec as P

EVERY = ("zlo", "core", "y", "zhi", "x")
GRP = ("y", "zhi", "x")
ARRIVED = 8 * 10**9
SWAP = [(0, 1), (1, 0)]
F32, BF16 = jnp.float32, jnp.bfloat16
VMEM = pl.BlockSpec(memory_space=pltpu.VMEM)
ANY = pl.BlockSpec(memory_space=pl.ANY)
SMEM = pl.BlockSpec(memory_space=pltpu.SMEM)
PARAMS = pltpu.CompilerParams(vmem_limit_bytes=40 * 1024 * 1024)


def passed_on(value, *hops):
    return lax.ppermute(value, "zlo", hops)


def spread(value, axis):
    count = lax.axis_size(axis)
    copies = jnp.broadcast_to(value[None], (count,) + value.shape)
    return lax.all_to_all(copies, axis, split_axis=0, concat_axis=0)


def copies_kernel(own_ref, other_ref, out_ref):
    share = own_ref.shape[0]
    for k in range(out_ref.shape[0]):
        out_ref[k, :share] = own_ref[...]
        out_ref[k, share:] = other_ref[...]


def arrived_kernel(far_ref, up_ref, down_ref, out_ref):
    out_ref[...] = jnp.zeros_like(out_ref)


def embed_kernel(
    place, arrived_ref, order_ref, gathered_ref, x0, up1, up2, far, down1, down2,
    half_ref, unit_ref, radius_ref, rows_ref, mapping,
):
    mapping[...] = jnp.dot(
        order_ref[...], gathered_ref[...], preferred_element_type=F32
    ).astype(BF16)
    blocks = ((x0, None), (up1, far), (up2, down2), (far, down1))
    for k, (low, high) in enumerate(blocks):
        rows = low.shape[0]
        at = pl.ds(k * rows, rows)
        block = low[...] if high is None else jnp.where(place[0] >= k, low[...], high[...])
        rows_ref[at, :] = block
        out = jnp.dot(block, mapping[...], preferred_element_type=F32)
        radius = jnp.sqrt(jnp.sum(out * out, axis=-1, keepdims=True) + 1e-06)
        unit = out / radius
        radius_ref[at, :] = radius
        unit_ref[at, :] = unit
        half_ref[at, :] = unit.astype(BF16)


def grad_kernel(
    own, grid, scalars, place, half_ref, partner_ref, unit_ref, radius_ref, rows_ref,
    local_ref, norms_ref, pre_ref, weights_ref,
):
    multiplier, offset = scalars[0], scalars[1]
    peers, held, columns = local_ref.shape
    start = pl.multiple_of((3 * place[0]) // 2 * 128, 128)
    total = None
    rows = 2 * own
    for k in range(rows_ref.shape[0] // rows):
        at = pl.ds(k * rows, rows)
        logits = multiplier * lax.dot_general(
            half_ref[at, :], partner_ref[...], (((1,), (1,)), ((), ())), preferred_element_type=F32
        ) + offset
        weights_ref[...] = (multiplier * jax.nn.sigmoid(logits)).astype(BF16)
        square = logits[:, k * rows : (k + 1) * rows]
        i = lax.broadcasted_iota(jnp.int32, square.shape, 0)
        j = lax.broadcasted_iota(jnp.int32, square.shape, 1)
        sign = jnp.where(j == jnp.where(i < own, i + own, i - own), 1.0, -1.0)
        weights_ref[:, at] = ((-multiplier * sign) * jax.nn.sigmoid(-sign * square)).astype(BF16)
        grad = jnp.dot(weights_ref[...], partner_ref[...], preferred_element_type=F32)
        unit = unit_ref[at, :]
        pre = (grad - unit * jnp.sum(unit * grad, axis=-1, keepdims=True)) / radius_ref[at, :]
        pre_ref[...] = pre
        if k == 0:
            wide = rows_ref[at, :].astype(F32)
            norms_ref[...] = jnp.sqrt(jnp.sum(wide * wide, axis=-1, keepdims=True)) * jnp.sqrt(
                jnp.sum(pre * pre, axis=-1, keepdims=True)
            )
        part = lax.dot_general(
            rows_ref[at, :],
            pre_ref[:, pl.ds(start, 256)].astype(BF16),
            (((0,), (0,)), ((), ())),
            preferred_element_type=F32,
        )
        total = part if total is None else total + part
    odd = place[0] % 2 == 1
    total = jnp.where(odd, total[:, 256 - columns :], total[:, :columns])
    n_y, n_zhi, n_x = grid
    share = held // n_zhi
    for k in range(peers * n_zhi):
        y, zhi, x = k // (n_zhi * n_x), k // n_x % n_zhi, k % n_x
        piece = total[k * share : (k + 1) * share].astype(BF16)
        local_ref[y * n_x + x, zhi * share : (zhi + 1) * share] = piece


def on_device(
    picture_inputs,
    caption_inputs,
    picture_mapping,
    caption_mapping,
    similarity_multiplier,
    score_constant,
):
    own, width = picture_inputs.shape
    share, embed = picture_mapping.shape
    first = lax.axis_index("core") == 0
    chips = lax.axis_size("zlo")
    n_y, n_zhi, n_x = (lax.axis_size(a) for a in GRP)
    piece = jnp.where(first, picture_mapping, caption_mapping)
    other = lax.ppermute(piece, "zhi", SWAP)
    mine = jnp.where(first, picture_inputs, caption_inputs)
    sent = jnp.where(first, caption_inputs, picture_inputs)
    chunk = jnp.concatenate([mine, lax.ppermute(sent, "core", SWAP)], axis=0)
    at_line = lax.axis_index("zlo")
    up1 = passed_on(chunk, (0, 1), (1, 2), (2, 3))
    down1 = passed_on(chunk, (1, 0), (2, 1), (3, 2))
    far = passed_on(jnp.where(at_line == 1, up1, down1), (1, 3), (2, 0))
    up2 = passed_on(up1, (1, 2), (2, 3))
    down2 = passed_on(down1, (1, 0), (2, 1))
    arrived = pl.pallas_call(
        arrived_kernel,
        out_shape=jax.ShapeDtypeStruct((8, 128), F32),
        in_specs=[ANY] * 3,
        out_specs=VMEM,
        cost_estimate=pl.CostEstimate(flops=ARRIVED, bytes_accessed=2**12, transcendentals=0),
    )(far, up2, down2)
    at_chip = at_line.astype(jnp.int32).reshape(1)
    copies = pl.pallas_call(
        copies_kernel,
        out_shape=jax.ShapeDtypeStruct((n_y, n_zhi * share, embed), BF16),
        in_specs=[VMEM] * 2,
        out_specs=VMEM,
        cost_estimate=pl.CostEstimate(flops=4 * 10**9, bytes_accessed=2**19, transcendentals=0),
    )(piece, other)
    near = lax.all_to_all(copies, "y", split_axis=0, concat_axis=0)
    near = near.reshape(n_y * n_zhi * share, embed)
    gathered = spread(near, "x").reshape(width, embed)
    at = jnp.arange(width, dtype=jnp.int32)
    owner, row = at // share, at % share
    at_half = (owner // n_x) % n_zhi
    at_half = jnp.where(lax.axis_index("zhi") == 0, at_half, 1 - at_half)
    from_row = (((owner % n_x) * n_y + owner // (n_x * n_zhi)) * n_zhi + at_half) * share + row
    order = (from_row[:, None] == at[None, :]).astype(BF16)
    rows = chips * chunk.shape[0]
    half, unit, radius, set_rows = pl.pallas_call(
        embed_kernel,
        out_shape=(
            jax.ShapeDtypeStruct((rows, embed), BF16),
            jax.ShapeDtypeStruct((rows, embed), F32),
            jax.ShapeDtypeStruct((rows, 1), F32),
            jax.ShapeDtypeStruct((rows, width), BF16),
        ),
        in_specs=[SMEM, ANY] + [VMEM] * 8,
        out_specs=(VMEM,) * 4,
        scratch_shapes=[pltpu.VMEM((width, embed), BF16)],
        compiler_params=PARAMS,
        cost_estimate=pl.CostEstimate(
            flops=2 * (rows + width) * width * embed, bytes_accessed=8 * 2**20, transcendentals=0
        ),
    )(
        at_chip, arrived, order, gathered, chunk, up1, up2, far, down1, down2
    )
    partner = lax.ppermute(half, "core", SWAP)
    columns = embed // chips
    local, norms = pl.pallas_call(
        functools.partial(grad_kernel, own, (n_y, n_zhi, n_x)),
        out_shape=(
            jax.ShapeDtypeStruct((n_y * n_x, n_zhi * share, columns), BF16),
            jax.ShapeDtypeStruct((2 * own, 1), F32),
        ),
        in_specs=[SMEM] * 2 + [VMEM] * 5,
        out_specs=(VMEM,) * 2,
        scratch_shapes=[pltpu.VMEM((2 * own, embed), F32), pltpu.VMEM((2 * own, rows), BF16)],
        compiler_params=PARAMS,
        cost_estimate=pl.CostEstimate(
            flops=4 * rows * rows * embed, bytes_accessed=8 * 2**20, transcendentals=rows * rows
        ),
    )(
        jnp.concatenate([similarity_multiplier, score_constant]),
        at_chip,
        half,
        partner,
        unit,
        radius,
        set_rows,
    )
    pieces = lax.all_to_all(local, ("y", "x"), split_axis=0, concat_axis=0, tiled=True)
    totals = jnp.sum(pieces.astype(F32), axis=0).reshape(n_zhi, 1, share, columns)
    totals = jnp.broadcast_to(totals, (n_zhi, 2 * chips, share, columns))
    parts = lax.all_to_all(
        totals.reshape(2 * n_zhi * chips, share, columns),
        ("zhi", "zlo", "core"),
        split_axis=0,
        concat_axis=0,
        tiled=True,
    )
    parts = parts.reshape(n_zhi, chips, 2, share, columns)
    img_proj_grad, txt_proj_grad = (
        jnp.concatenate([jnp.sum(parts[:, z, side], axis=0) for z in range(chips)], axis=1)
        for side in range(2)
    )
    norms = norms.reshape(2 * own)
    own_norms = norms[:own]
    their_norms = lax.ppermute(norms[own:], "core", SWAP)
    img_norms = jnp.where(first, own_norms, their_norms)
    txt_norms = jnp.where(first, their_norms, own_norms)
    return (img_proj_grad, txt_proj_grad, img_norms, txt_norms)


def build(fine):
    in_specs = (P(EVERY, None), P(EVERY, None), P(GRP, None), P(GRP, None), P(), P())
    out_specs = (P(GRP, None), P(GRP, None), P(EVERY), P(EVERY))
    return jax.shard_map(
        on_device, mesh=fine, in_specs=in_specs, out_specs=out_specs, check_vma=False
    )


def solution(mesh):
    return build(Mesh(mesh.devices.reshape(4, 2, 8, 2, 4), EVERY))
```

```python
import functools

import jax
import jax.numpy as jnp
from jax import lax
from jax.experimental import pallas as pl
from jax.experimental.pallas import tpu as pltpu
from jax.sharding import Mesh, PartitionSpec as P

EVERY = ("zlo", "core", "y", "zhi", "x")
GRP = ("y", "zhi", "x")
ARRIVED = 8 * 10**9
SWAP = [(0, 1), (1, 0)]
F32, BF16 = jnp.float32, jnp.bfloat16
VMEM = pl.BlockSpec(memory_space=pltpu.VMEM)
ANY = pl.BlockSpec(memory_space=pl.ANY)
SMEM = pl.BlockSpec(memory_space=pltpu.SMEM)
PARAMS = pltpu.CompilerParams(vmem_limit_bytes=40 * 1024 * 1024)


def passed_on(value, *hops):
    return lax.ppermute(value, "zlo", hops)


def spread(value, axis):
    count = lax.axis_size(axis)
    copies = jnp.broadcast_to(value[None], (count,) + value.shape)
    return lax.all_to_all(copies, axis, split_axis=0, concat_axis=0)


def copies_kernel(own_ref, other_ref, out_ref):
    share = own_ref.shape[0]
    for k in range(out_ref.shape[0]):
        out_ref[k, :share] = own_ref[...]
        out_ref[k, share:] = other_ref[...]


def arrived_kernel(far_ref, up_ref, out_ref):
    out_ref[...] = jnp.zeros_like(out_ref)


def embed_kernel(
    place, arrived_ref, order_ref, gathered_ref, x0, up1, up2, far, down1, down2,
    half_ref, unit_ref, radius_ref, rows_ref, mapping,
):
    mapping[...] = jnp.dot(
        order_ref[...], gathered_ref[...], preferred_element_type=F32
    ).astype(BF16)
    blocks = ((x0, None), (up1, far), (up2, down2), (far, down1))
    for k, (low, high) in enumerate(blocks):
        rows = low.shape[0]
        at = pl.ds(k * rows, rows)
        block = low[...] if high is None else jnp.where(place[0] >= k, low[...], high[...])
        rows_ref[at, :] = block
        out = jnp.dot(block, mapping[...], preferred_element_type=F32)
        radius = jnp.sqrt(jnp.sum(out * out, axis=-1, keepdims=True) + 1e-06)
        unit = out / radius
        radius_ref[at, :] = radius
        unit_ref[at, :] = unit
        half_ref[at, :] = unit.astype(BF16)


def grad_kernel(
    own, grid, scalars, place, half_ref, partner_ref, unit_ref, radius_ref, rows_ref,
    local_ref, norms_ref, pre_ref, weights_ref,
):
    multiplier, offset = scalars[0], scalars[1]
    peers, held, columns = local_ref.shape
    start = pl.multiple_of((3 * place[0]) // 2 * 128, 128)
    total = None
    rows = 2 * own
    for k in range(rows_ref.shape[0] // rows):
        at = pl.ds(k * rows, rows)
        logits = multiplier * lax.dot_general(
            half_ref[at, :], partner_ref[...], (((1,), (1,)), ((), ())), preferred_element_type=F32
        ) + offset
        weights_ref[...] = (multiplier * jax.nn.sigmoid(logits)).astype(BF16)
        square = logits[:, k * rows : (k + 1) * rows]
        i = lax.broadcasted_iota(jnp.int32, square.shape, 0)
        j = lax.broadcasted_iota(jnp.int32, square.shape, 1)
        sign = jnp.where(j == jnp.where(i < own, i + own, i - own), 1.0, -1.0)
        weights_ref[:, at] = ((-multiplier * sign) * jax.nn.sigmoid(-sign * square)).astype(BF16)
        grad = jnp.dot(weights_ref[...], partner_ref[...], preferred_element_type=F32)
        unit = unit_ref[at, :]
        pre = (grad - unit * jnp.sum(unit * grad, axis=-1, keepdims=True)) / radius_ref[at, :]
        pre_ref[...] = pre
        if k == 0:
            wide = rows_ref[at, :].astype(F32)
            norms_ref[...] = jnp.sqrt(jnp.sum(wide * wide, axis=-1, keepdims=True)) * jnp.sqrt(
                jnp.sum(pre * pre, axis=-1, keepdims=True)
            )
        part = lax.dot_general(
            rows_ref[at, :],
            pre_ref[:, pl.ds(start, 256)].astype(BF16),
            (((0,), (0,)), ((), ())),
            preferred_element_type=F32,
        )
        total = part if total is None else total + part
    odd = place[0] % 2 == 1
    total = jnp.where(odd, total[:, 256 - columns :], total[:, :columns])
    n_y, n_zhi, n_x = grid
    share = held // n_zhi
    for k in range(peers * n_zhi):
        y, zhi, x = k // (n_zhi * n_x), k // n_x % n_zhi, k % n_x
        piece = total[k * share : (k + 1) * share].astype(BF16)
        local_ref[y * n_x + x, zhi * share : (zhi + 1) * share] = piece


def on_device(
    picture_inputs,
    caption_inputs,
    picture_mapping,
    caption_mapping,
    similarity_multiplier,
    score_constant,
):
    own, width = picture_inputs.shape
    share, embed = picture_mapping.shape
    first = lax.axis_index("core") == 0
    chips = lax.axis_size("zlo")
    n_y, n_zhi, n_x = (lax.axis_size(a) for a in GRP)
    piece = jnp.where(first, picture_mapping, caption_mapping)
    other = lax.ppermute(piece, "zhi", SWAP)
    mine = jnp.where(first, picture_inputs, caption_inputs)
    sent = jnp.where(first, caption_inputs, picture_inputs)
    chunk = jnp.concatenate([mine, lax.ppermute(sent, "core", SWAP)], axis=0)
    at_line = lax.axis_index("zlo")
    up1 = passed_on(chunk, (0, 1), (1, 2), (2, 3))
    down1 = passed_on(chunk, (1, 0), (2, 1), (3, 2))
    far = passed_on(jnp.where(at_line == 1, up1, down1), (1, 3), (2, 0))
    up2 = passed_on(up1, (1, 2), (2, 3))
    down2 = passed_on(down1, (1, 0), (2, 1))
    arrived = pl.pallas_call(
        arrived_kernel,
        out_shape=jax.ShapeDtypeStruct((8, 128), F32),
        in_specs=[ANY] * 2,
        out_specs=VMEM,
        cost_estimate=pl.CostEstimate(flops=ARRIVED, bytes_accessed=2**12, transcendentals=0),
    )(far, up2)
    at_chip = at_line.astype(jnp.int32).reshape(1)
    copies = pl.pallas_call(
        copies_kernel,
        out_shape=jax.ShapeDtypeStruct((n_y, n_zhi * share, embed), BF16),
        in_specs=[VMEM] * 2,
        out_specs=VMEM,
        cost_estimate=pl.CostEstimate(flops=4 * 10**9, bytes_accessed=2**19, transcendentals=0),
    )(piece, other)
    near = lax.all_to_all(copies, "y", split_axis=0, concat_axis=0)
    near = near.reshape(n_y * n_zhi * share, embed)
    gathered = spread(near, "x").reshape(width, embed)
    at = jnp.arange(width, dtype=jnp.int32)
    owner, row = at // share, at % share
    at_half = (owner // n_x) % n_zhi
    at_half = jnp.where(lax.axis_index("zhi") == 0, at_half, 1 - at_half)
    from_row = (((owner % n_x) * n_y + owner // (n_x * n_zhi)) * n_zhi + at_half) * share + row
    order = (from_row[:, None] == at[None, :]).astype(BF16)
    rows = chips * chunk.shape[0]
    half, unit, radius, set_rows = pl.pallas_call(
        embed_kernel,
        out_shape=(
            jax.ShapeDtypeStruct((rows, embed), BF16),
            jax.ShapeDtypeStruct((rows, embed), F32),
            jax.ShapeDtypeStruct((rows, 1), F32),
            jax.ShapeDtypeStruct((rows, width), BF16),
        ),
        in_specs=[SMEM, ANY] + [VMEM] * 8,
        out_specs=(VMEM,) * 4,
        scratch_shapes=[pltpu.VMEM((width, embed), BF16)],
        compiler_params=PARAMS,
        cost_estimate=pl.CostEstimate(
            flops=2 * (rows + width) * width * embed, bytes_accessed=8 * 2**20, transcendentals=0
        ),
    )(
        at_chip, arrived, order, gathered, chunk, up1, up2, far, down1, down2
    )
    partner = lax.ppermute(half, "core", SWAP)
    columns = embed // chips
    local, norms = pl.pallas_call(
        functools.partial(grad_kernel, own, (n_y, n_zhi, n_x)),
        out_shape=(
            jax.ShapeDtypeStruct((n_y * n_x, n_zhi * share, columns), BF16),
            jax.ShapeDtypeStruct((2 * own, 1), F32),
        ),
        in_specs=[SMEM] * 2 + [VMEM] * 5,
        out_specs=(VMEM,) * 2,
        scratch_shapes=[pltpu.VMEM((2 * own, embed), F32), pltpu.VMEM((2 * own, rows), BF16)],
        compiler_params=PARAMS,
        cost_estimate=pl.CostEstimate(
            flops=4 * rows * rows * embed, bytes_accessed=8 * 2**20, transcendentals=rows * rows
        ),
    )(
        jnp.concatenate([similarity_multiplier, score_constant]),
        at_chip,
        half,
        partner,
        unit,
        radius,
        set_rows,
    )
    pieces = lax.all_to_all(local, ("y", "x"), split_axis=0, concat_axis=0, tiled=True)
    totals = jnp.sum(pieces.astype(F32), axis=0).reshape(n_zhi, 1, share, columns)
    totals = jnp.broadcast_to(totals, (n_zhi, 2 * chips, share, columns))
    parts = lax.all_to_all(
        totals.reshape(2 * n_zhi * chips, share, columns),
        ("zhi", "zlo", "core"),
        split_axis=0,
        concat_axis=0,
        tiled=True,
    )
    parts = parts.reshape(n_zhi, chips, 2, share, columns)
    img_proj_grad, txt_proj_grad = (
        jnp.concatenate([jnp.sum(parts[:, z, side], axis=0) for z in range(chips)], axis=1)
        for side in range(2)
    )
    norms = norms.reshape(2 * own)
    own_norms = norms[:own]
    their_norms = lax.ppermute(norms[own:], "core", SWAP)
    img_norms = jnp.where(first, own_norms, their_norms)
    txt_norms = jnp.where(first, their_norms, own_norms)
    return (img_proj_grad, txt_proj_grad, img_norms, txt_norms)


def build(fine):
    in_specs = (P(EVERY, None), P(EVERY, None), P(GRP, None), P(GRP, None), P(), P())
    out_specs = (P(GRP, None), P(GRP, None), P(EVERY), P(EVERY))
    return jax.shard_map(
        on_device, mesh=fine, in_specs=in_specs, out_specs=out_specs, check_vma=False
    )


def solution(mesh):
    return build(Mesh(mesh.devices.reshape(4, 2, 8, 2, 4), EVERY))
```

```python
import functools

import jax
import jax.numpy as jnp
from jax import lax
from jax.experimental import pallas as pl
from jax.experimental.pallas import tpu as pltpu
from jax.sharding import Mesh, PartitionSpec as P

EVERY = ("zlo", "core", "y", "zhi", "x")
GRP = ("y", "zhi", "x")
ARRIVED = 8 * 10**9
SWAP = [(0, 1), (1, 0)]
F32, BF16 = jnp.float32, jnp.bfloat16
VMEM = pl.BlockSpec(memory_space=pltpu.VMEM)
ANY = pl.BlockSpec(memory_space=pl.ANY)
SMEM = pl.BlockSpec(memory_space=pltpu.SMEM)
PARAMS = pltpu.CompilerParams(vmem_limit_bytes=40 * 1024 * 1024)


def passed_on(value, *hops):
    return lax.ppermute(value, "zlo", hops)


def spread(value, axis):
    count = lax.axis_size(axis)
    copies = jnp.broadcast_to(value[None], (count,) + value.shape)
    return lax.all_to_all(copies, axis, split_axis=0, concat_axis=0)


def copies_kernel(own_ref, other_ref, out_ref):
    share = own_ref.shape[0]
    for k in range(out_ref.shape[0]):
        out_ref[k, :share] = own_ref[...]
        out_ref[k, share:] = other_ref[...]


def arrived_kernel(far_ref, up_ref, out_ref):
    out_ref[...] = jnp.zeros_like(out_ref)


def embed_kernel(
    place, arrived_ref, order_ref, gathered_ref, x0, up1, up2, far, down1, down2,
    half_ref, unit_ref, inverse_ref, rows_ref, mapping,
):
    mapping[...] = jnp.dot(
        order_ref[...], gathered_ref[...], preferred_element_type=F32
    ).astype(BF16)
    blocks = ((x0, None), (up1, far), (up2, down2), (far, down1))
    for k, (low, high) in enumerate(blocks):
        rows = low.shape[0]
        at = pl.ds(k * rows, rows)
        block = low[...] if high is None else jnp.where(place[0] >= k, low[...], high[...])
        rows_ref[at, :] = block
        out = jnp.dot(block, mapping[...], preferred_element_type=F32)
        radius = jnp.sqrt(jnp.sum(out * out, axis=-1, keepdims=True) + 1e-06)
        inverse = 1.0 / radius
        unit = out * inverse
        inverse_ref[at, :] = inverse
        unit_ref[at, :] = unit
        half_ref[at, :] = unit.astype(BF16)


def grad_kernel(
    own, grid, scalars, place, half_ref, partner_ref, unit_ref, inverse_ref, rows_ref,
    local_ref, norms_ref, pre_ref, weights_ref,
):
    multiplier, offset = scalars[0], scalars[1]
    peers, held, columns = local_ref.shape
    start = pl.multiple_of((3 * place[0]) // 2 * 128, 128)
    total = None
    rows = 2 * own
    for k in range(rows_ref.shape[0] // rows):
        at = pl.ds(k * rows, rows)
        logits = multiplier * lax.dot_general(
            half_ref[at, :], partner_ref[...], (((1,), (1,)), ((), ())), preferred_element_type=F32
        ) + offset
        weights_ref[...] = (multiplier * jax.nn.sigmoid(logits)).astype(BF16)
        square = logits[:, k * rows : (k + 1) * rows]
        i = lax.broadcasted_iota(jnp.int32, square.shape, 0)
        j = lax.broadcasted_iota(jnp.int32, square.shape, 1)
        sign = jnp.where(j == jnp.where(i < own, i + own, i - own), 1.0, -1.0)
        weights_ref[:, at] = ((-multiplier * sign) * jax.nn.sigmoid(-sign * square)).astype(BF16)
        grad = jnp.dot(weights_ref[...], partner_ref[...], preferred_element_type=F32)
        unit = unit_ref[at, :]
        pre = (grad - unit * jnp.sum(unit * grad, axis=-1, keepdims=True)) * inverse_ref[at, :]
        pre_ref[...] = pre
        if k == 0:
            wide = rows_ref[at, :].astype(F32)
            norms_ref[...] = jnp.sqrt(jnp.sum(wide * wide, axis=-1, keepdims=True)) * jnp.sqrt(
                jnp.sum(pre * pre, axis=-1, keepdims=True)
            )
        part = lax.dot_general(
            rows_ref[at, :],
            pre_ref[:, pl.ds(start, 256)].astype(BF16),
            (((0,), (0,)), ((), ())),
            preferred_element_type=F32,
        )
        total = part if total is None else total + part
    odd = place[0] % 2 == 1
    total = jnp.where(odd, total[:, 256 - columns :], total[:, :columns])
    n_y, n_zhi, n_x = grid
    share = held // n_zhi
    for k in range(peers * n_zhi):
        y, zhi, x = k // (n_zhi * n_x), k // n_x % n_zhi, k % n_x
        piece = total[k * share : (k + 1) * share].astype(BF16)
        local_ref[y * n_x + x, zhi * share : (zhi + 1) * share] = piece


def on_device(
    picture_inputs,
    caption_inputs,
    picture_mapping,
    caption_mapping,
    similarity_multiplier,
    score_constant,
):
    own, width = picture_inputs.shape
    share, embed = picture_mapping.shape
    first = lax.axis_index("core") == 0
    chips = lax.axis_size("zlo")
    n_y, n_zhi, n_x = (lax.axis_size(a) for a in GRP)
    piece = jnp.where(first, picture_mapping, caption_mapping)
    other = lax.ppermute(piece, "zhi", SWAP)
    mine = jnp.where(first, picture_inputs, caption_inputs)
    sent = jnp.where(first, caption_inputs, picture_inputs)
    chunk = jnp.concatenate([mine, lax.ppermute(sent, "core", SWAP)], axis=0)
    at_line = lax.axis_index("zlo")
    up1 = passed_on(chunk, (0, 1), (1, 2), (2, 3))
    down1 = passed_on(chunk, (1, 0), (2, 1), (3, 2))
    far = passed_on(jnp.where(at_line == 1, up1, down1), (1, 3), (2, 0))
    up2 = passed_on(up1, (1, 2), (2, 3))
    down2 = passed_on(down1, (1, 0), (2, 1))
    arrived = pl.pallas_call(
        arrived_kernel,
        out_shape=jax.ShapeDtypeStruct((8, 128), F32),
        in_specs=[ANY] * 2,
        out_specs=VMEM,
        cost_estimate=pl.CostEstimate(flops=ARRIVED, bytes_accessed=2**12, transcendentals=0),
    )(far, up2)
    at_chip = at_line.astype(jnp.int32).reshape(1)
    copies = pl.pallas_call(
        copies_kernel,
        out_shape=jax.ShapeDtypeStruct((n_y, n_zhi * share, embed), BF16),
        in_specs=[VMEM] * 2,
        out_specs=VMEM,
        cost_estimate=pl.CostEstimate(flops=4 * 10**9, bytes_accessed=2**19, transcendentals=0),
    )(piece, other)
    near = lax.all_to_all(copies, "y", split_axis=0, concat_axis=0)
    near = near.reshape(n_y * n_zhi * share, embed)
    gathered = spread(near, "x").reshape(width, embed)
    at = jnp.arange(width, dtype=jnp.int32)
    owner, row = at // share, at % share
    at_half = (owner // n_x) % n_zhi
    at_half = jnp.where(lax.axis_index("zhi") == 0, at_half, 1 - at_half)
    from_row = (((owner % n_x) * n_y + owner // (n_x * n_zhi)) * n_zhi + at_half) * share + row
    order = (from_row[:, None] == at[None, :]).astype(BF16)
    rows = chips * chunk.shape[0]
    half, unit, inverse, set_rows = pl.pallas_call(
        embed_kernel,
        out_shape=(
            jax.ShapeDtypeStruct((rows, embed), BF16),
            jax.ShapeDtypeStruct((rows, embed), F32),
            jax.ShapeDtypeStruct((rows, 1), F32),
            jax.ShapeDtypeStruct((rows, width), BF16),
        ),
        in_specs=[SMEM, ANY] + [VMEM] * 8,
        out_specs=(VMEM,) * 4,
        scratch_shapes=[pltpu.VMEM((width, embed), BF16)],
        compiler_params=PARAMS,
        cost_estimate=pl.CostEstimate(
            flops=2 * (rows + width) * width * embed, bytes_accessed=8 * 2**20, transcendentals=0
        ),
    )(
        at_chip, arrived, order, gathered, chunk, up1, up2, far, down1, down2
    )
    partner = lax.ppermute(half, "core", SWAP)
    columns = embed // chips
    local, norms = pl.pallas_call(
        functools.partial(grad_kernel, own, (n_y, n_zhi, n_x)),
        out_shape=(
            jax.ShapeDtypeStruct((n_y * n_x, n_zhi * share, columns), BF16),
            jax.ShapeDtypeStruct((2 * own, 1), F32),
        ),
        in_specs=[SMEM] * 2 + [VMEM] * 5,
        out_specs=(VMEM,) * 2,
        scratch_shapes=[pltpu.VMEM((2 * own, embed), F32), pltpu.VMEM((2 * own, rows), BF16)],
        compiler_params=PARAMS,
        cost_estimate=pl.CostEstimate(
            flops=4 * rows * rows * embed, bytes_accessed=8 * 2**20, transcendentals=rows * rows
        ),
    )(
        jnp.concatenate([similarity_multiplier, score_constant]),
        at_chip,
        half,
        partner,
        unit,
        inverse,
        set_rows,
    )
    pieces = lax.all_to_all(local, ("y", "x"), split_axis=0, concat_axis=0, tiled=True)
    totals = jnp.sum(pieces.astype(F32), axis=0).reshape(n_zhi, 1, share, columns)
    totals = jnp.broadcast_to(totals, (n_zhi, 2 * chips, share, columns))
    parts = lax.all_to_all(
        totals.reshape(2 * n_zhi * chips, share, columns),
        ("zhi", "zlo", "core"),
        split_axis=0,
        concat_axis=0,
        tiled=True,
    )
    parts = parts.reshape(n_zhi, chips, 2, share, columns)
    img_proj_grad, txt_proj_grad = (
        jnp.concatenate([jnp.sum(parts[:, z, side], axis=0) for z in range(chips)], axis=1)
        for side in range(2)
    )
    norms = norms.reshape(2 * own)
    own_norms = norms[:own]
    their_norms = lax.ppermute(norms[own:], "core", SWAP)
    img_norms = jnp.where(first, own_norms, their_norms)
    txt_norms = jnp.where(first, their_norms, own_norms)
    return (img_proj_grad, txt_proj_grad, img_norms, txt_norms)


def build(fine):
    in_specs = (P(EVERY, None), P(EVERY, None), P(GRP, None), P(GRP, None), P(), P())
    out_specs = (P(GRP, None), P(GRP, None), P(EVERY), P(EVERY))
    return jax.shard_map(
        on_device, mesh=fine, in_specs=in_specs, out_specs=out_specs, check_vma=False
    )


def solution(mesh):
    return build(Mesh(mesh.devices.reshape(4, 2, 8, 2, 4), EVERY))
```
